128 devices in a mesh: elem: 32 (over y, x, core), mode: 4 (over z).
Axes of the slice: x: 4, y: 4, z: 4, core: 2. Of those that a mesh axis runs over, the one named last changes fastest.
Arguments:
- velocity: float32 [3, 20736, 2, 512], P(None, 'elem', None, 'mode'), may hold values from -3 to 3
- column_width: float32 [32], P('elem'), may hold values from 0.5 to 2
- row_height: float32 [8], replicated, may hold values from 0.5 to 2
- disc_mask: int32 [256], P('elem'), may hold values from 0 to 1, as said below
Outputs:
- velocity_new: float32 [3, 20736, 2, 512], P(None, 'elem', None, 'mode')
The draws below stay inside these ranges and needn't reach their ends.
Inputs may be any that keep to these rules, and one draw needn't show every extreme that they name: `disc_mask`: in each column of 8 elements the ones form one run of 2 to 4 consecutive rows, counted cyclically in y.
All inputs are finite; a program needn't handle non-finite values.
Results may differ from the reference program's by a relative error of at most 0.0001.
Values sent between devices are 32-bit elements; how exact they have to be, the bound alone decides.
No kernel may reach another device: no remote copies, remote signals or barrier semaphores. Data moves between devices by JAX's collectives and lax.ppermute only.
A program may use at most 128 MiB of HBM per device.

```python
import math
import jax
import jax.numpy as jnp
import numpy as np
from jax import lax

ORDER = 8
MODES = 512
E_DEV = 8
ITERS = 2
COLS = 32
ELEMS = 256
NODES = 20736


def draw_disc_mask(key, part):
    key_start, key_length = jax.random.split(key)
    starts = jax.random.randint(key_start, (COLS,), 0, E_DEV)
    lengths = jax.random.randint(key_length, (COLS,), 2, 5)
    column_index = jnp.arange(COLS)
    lengths = jnp.where(column_index == 0, 4, jnp.where(column_index == 1, 2, lengths))
    row_index = jnp.arange(E_DEV)
    marked = (row_index[None, :] - starts[:, None]) % E_DEV < lengths[:, None]
    return marked.astype(jnp.int32).reshape(ELEMS)


def steps_of(rng, shape, shards, low, high):
    loudness, own = 1.0, jax.random.fold_in(rng, 6)
    for position, blocks in shards:
        heights = jnp.exp(jax.random.uniform(jax.random.fold_in(own, position), (blocks,), jnp.float32, low / len(shards), high / len(shards)))
        loudness = loudness * jnp.repeat(heights, shape[position] // blocks).reshape([-1 if axis == position else 1 for axis in range(len(shape))])
    return loudness


def gaussian(own_key, dims, scale, reach, cuts=(), held_as=jnp.bfloat16):
    values = jax.random.normal(own_key, dims, jnp.float32) * scale
    if len(cuts) > 0:
        values = steps_of(own_key, dims, cuts, -0.22, 0.18) * values
    return jnp.clip(values, min=-reach, max=reach).astype(held_as)


def setup_inputs(seed: int = 0) -> dict:
    key_of = jax.random.split(jax.random.key(seed), 5)
    velocity = gaussian(key_of[0], (3, NODES, 2, MODES), 0.5, 3.0, ((1, 32), (3, 4)), jnp.float32)
    column_width = jnp.clip(jnp.exp(math.log(2.0) - 1.3862944 * jax.random.uniform(key_of[1], (COLS,), jnp.float32) ** steps_of(key_of[1], (COLS,), ((0, 32),), -0.2, 0.2)), 0.5, 2.0)
    row_height = jnp.clip(jnp.exp(jax.random.uniform(key_of[2], (E_DEV,), jnp.float32, math.log(0.5), math.log(2.0))), 0.5, 2.0)
    disc_mask = draw_disc_mask(jax.random.fold_in(key_of[4], 71), 0)
    return dict(velocity=velocity, column_width=column_width, row_height=row_height, disc_mask=disc_mask)


gll_points = [-1.0, -0.8997579954114602, -0.6771862795107377, -0.3631174638261782, 0.0, 0.3631174638261782, 0.6771862795107377, 0.8997579954114602, 1.0]
gll_weights = [0.0277777777777778, 0.1654953615608055, 0.2745387125001617, 0.3464285109730463, 0.3715192743764172, 0.3464285109730463, 0.2745387125001617, 0.1654953615608055, 0.0277777777777778]
viscosity = 0.5
time_step = 0.02
thrust_coef = 4.0 / 3.0
highest = lax.Precision.HIGHEST

def node_tables():
    points = np.array(gll_points)
    identity = np.eye(9)
    differences = points[:, None] - points[None, :] + identity
    barycentric = 1.0 / np.prod(differences, axis=1)
    off_diagonal = barycentric[None, :] / barycentric[:, None] / differences * (1.0 - identity)
    derivative = off_diagonal - identity * off_diagonal.sum(axis=1)[:, None]
    return (jnp.asarray(derivative, dtype=jnp.float32), jnp.asarray(np.array(gll_weights), dtype=jnp.float32))

def spectral_tables(mode_count):
    planes = 3 * mode_count
    wave_index = jnp.arange(mode_count, dtype=jnp.int32)
    plane_index = jnp.arange(planes, dtype=jnp.int32)
    phase_index = wave_index[:, None] * plane_index[None, :] % planes
    angles = 2.0 * math.pi / planes * phase_index.astype(jnp.float32)
    cosine_table = jnp.cos(angles)
    sine_table = jnp.sin(angles)
    mode_weight = jnp.where(wave_index == 0, 1.0, 2.0).astype(jnp.float32)[:, None] / math.sqrt(mode_count)
    wave_number = 8.0 / mode_count * wave_index.astype(jnp.float32)[:, None]
    inverse = jnp.concatenate([mode_weight * cosine_table, -mode_weight * sine_table], axis=0)
    spanwise = jnp.concatenate([-wave_number * mode_weight * sine_table, -wave_number * mode_weight * cosine_table], axis=0)
    forward = math.sqrt(mode_count) / planes * jnp.concatenate([cosine_table, -sine_table], axis=0).T
    return (inverse, spanwise, forward)

def assemble(nodal_field):
    upper_layer = nodal_field[:, :, :, 8] + jnp.roll(nodal_field[:, :, :, 0], -1, axis=1)
    nodal_field = jnp.concatenate([jnp.roll(upper_layer, 1, axis=1)[:, :, :, None], nodal_field[:, :, :, 1:8], upper_layer[:, :, :, None]], axis=3)
    upper_layer = nodal_field[:, :, :, :, 8] + jnp.roll(nodal_field[:, :, :, :, 0], -1, axis=2)
    return jnp.concatenate([jnp.roll(upper_layer, 1, axis=2)[:, :, :, :, None], nodal_field[:, :, :, :, 1:8], upper_layer[:, :, :, :, None]], axis=4)

def apply_operator(nodal_field, derivative, quad_weights, ratio_x, ratio_y, jacobian, factor):
    grad_r = jnp.einsum('ij,pcejbl->pceibl', derivative, nodal_field, precision=highest)
    grad_s = jnp.einsum('ij,pceajl->pceail', derivative, nodal_field, precision=highest)
    flux_r = grad_r * quad_weights[None, None, None, :, :, None] * ratio_x[None, :, :, None, None, None]
    flux_s = grad_s * quad_weights[None, None, None, :, :, None] * ratio_y[None, :, :, None, None, None]
    stiffness = jnp.einsum('ji,pcejbl->pceibl', derivative, flux_r, precision=highest) + jnp.einsum('ji,pceajl->pceail', derivative, flux_s, precision=highest)
    masses = jacobian[None, :, :, None, None, None] * quad_weights[None, None, None, :, :, None] * nodal_field
    return assemble(factor * masses + viscosity * stiffness)

def weighted_sum(left_field, right_field, multiplicity):
    return lax.optimization_barrier(jnp.sum(left_field * right_field * multiplicity[None, None, None, :, :, None], axis=(1, 2, 3, 4)))

def reference(velocity, column_width, row_height, disc_mask):
    derivative, weights = node_tables()
    quad_weights = weights[:, None] * weights[None, :]
    node_index = jnp.arange(9)
    edge_count = jnp.where((node_index == 0) | (node_index == 8), 2.0, 1.0).astype(jnp.float32)
    multiplicity = 1.0 / (edge_count[:, None] * edge_count[None, :])
    planes = 3 * MODES
    inverse, spanwise, forward = spectral_tables(MODES)
    nodal_field = velocity.reshape(3, COLS, E_DEV, 9, 9, 2 * MODES)
    wavenumber = 8.0 / MODES * jnp.arange(MODES).astype(jnp.float32)
    plane_index = jnp.arange(planes)
    in_disc = ((plane_index >= 3 * planes // 8) & (plane_index < 5 * planes // 8)).astype(jnp.float32)
    disc_planes = 5 * planes // 8 - 3 * planes // 8
    disc_float = disc_mask.astype(jnp.float32).reshape(COLS, E_DEV)

    def column_tendency(inputs):
        column, col_width, disc_rows = inputs
        values = jnp.einsum('peabl,lq->peabq', column, inverse, precision=highest)
        along_z = jnp.einsum('peabl,lq->peabq', column, spanwise, precision=highest)
        along_x = 2.0 / col_width * jnp.einsum('ij,pejbq->peibq', derivative, values, precision=highest)
        along_y = (2.0 / row_height)[None, :, None, None, None] * jnp.einsum('ij,peajq->peaiq', derivative, values, precision=highest)
        advection = values[0][None] * along_x + values[1][None] * along_y + values[2][None] * along_z
        jacobian = col_width * row_height / 4.0
        node_weight = (disc_rows * jacobian)[:, None, None] * quad_weights[None]
        disc_total = jnp.sum(node_weight[:, :, :, None] * values[0] * values[0] * in_disc)
        disc_area = disc_planes * col_width * jnp.sum(disc_rows * row_height)
        pressure = disc_total / disc_area
        thrust = -(0.5 * thrust_coef * ORDER) * pressure / col_width * disc_rows[:, None, None, None] * in_disc
        tendency = jnp.concatenate([(thrust - advection[0])[None], -advection[1:]], axis=0)
        return jnp.einsum('peabq,ql->peabl', tendency, forward, precision=highest)
    columns = jnp.moveaxis(nodal_field, 1, 0)
    tendencies = lax.map(column_tendency, (columns, column_width, disc_float))
    tendency = jnp.moveaxis(tendencies, 0, 1)
    u_star = nodal_field + time_step * tendency
    jacobian = column_width[:, None] * row_height[None, :] / 4.0
    ratio_x = row_height[None, :] / column_width[:, None]
    ratio_y = column_width[:, None] / row_height[None, :]
    single = 1.0 / time_step + viscosity * wavenumber * wavenumber
    factor = jnp.concatenate([single, single])
    right_side = assemble(jacobian[None, :, :, None, None, None] * quad_weights[None, None, None, :, :, None] * u_star) / time_step
    residual = right_side
    direction = right_side
    solution = jnp.zeros_like(right_side)
    norm_now = weighted_sum(residual, residual, multiplicity)
    for iteration in range(ITERS):
        image_field = apply_operator(direction, derivative, quad_weights, ratio_x, ratio_y, jacobian, factor)
        step_size = (norm_now / weighted_sum(direction, image_field, multiplicity))[:, None, None, None, None, :]
        solution = solution + step_size * direction
        residual = residual - step_size * image_field
        if iteration + 1 < ITERS:
            norm_next = weighted_sum(residual, residual, multiplicity)
            direction = residual + (norm_next / norm_now)[:, None, None, None, None, :] * direction
            norm_now = norm_next
    return solution.reshape(3, NODES, 2, MODES)
```

```python
import math

import jax
import jax.numpy as jnp
import ml_dtypes
import numpy as np
from jax import lax
from jax.experimental import pallas as pl
from jax.experimental.pallas import tpu as pltpu
from jax.sharding import PartitionSpec as P

ORDER = 8
N1 = ORDER + 1
NN = N1 * N1

gll_points = [
    -1.0,
    -0.8997579954114602,
    -0.6771862795107377,
    -0.3631174638261782,
    0.0,
    0.3631174638261782,
    0.6771862795107377,
    0.8997579954114602,
    1.0,
]
gll_weights = [
    0.0277777777777778,
    0.1654953615608055,
    0.2745387125001617,
    0.3464285109730463,
    0.3715192743764172,
    0.3464285109730463,
    0.2745387125001617,
    0.1654953615608055,
    0.0277777777777778,
]
viscosity = 0.5
time_step = 0.02
thrust_coef = 4.0 / 3.0

MODES = 512
PLANES = 3 * MODES
HALF = PLANES // 2
GROUPS = 4
LOCAL = MODES // GROUPS
ROWS = 8
COLUMNS = 32
NODES = ROWS * NN
SHARE = NODES // GROUPS
PAD = 168
TILE = 256
FORWARD = math.sqrt(MODES) / PLANES
DISC_LO = 3 * PLANES // 8
DISC_HI = 5 * PLANES // 8
VMEM_LIMIT = 56 * 1024 * 1024
F32 = jnp.float32
BF16 = jnp.bfloat16


def derivative_matrix():
    points = np.array(gll_points)
    identity = np.eye(9)
    differences = points[:, None] - points[None, :] + identity
    barycentric = 1.0 / np.prod(differences, axis=1)
    off_diagonal = barycentric[None, :] / barycentric[:, None] / differences * (1.0 - identity)
    return off_diagonal - identity * off_diagonal.sum(axis=1)[:, None]


W1 = np.array(gll_weights)
D1 = derivative_matrix()
K1 = (D1.T @ (W1[:, None] * D1)) / W1[:, None]
MULT = np.ones(9)
MULT[0] = MULT[8] = 0.5


def split_table(table):
    table = np.asarray(table, np.float32)
    high = table.astype(ml_dtypes.bfloat16)
    low = (table - high.astype(np.float32)).astype(ml_dtypes.bfloat16)
    return jnp.asarray(high), jnp.asarray(low)


def plane_tables():
    k = np.arange(MODES)[:, None]
    j = np.arange(HALF)[None, :]
    angle = 2.0 * np.pi / PLANES * ((k * j) % PLANES)
    return split_table(np.cos(angle)) + split_table(np.sin(angle))


def gradient_table():
    one = np.eye(9)
    along_x = np.kron(np.eye(2), np.kron(D1, one))
    along_y = np.kron(np.eye(2), np.kron(one, D1))
    table = np.zeros((2 * PAD, PAD))
    table[:SHARE, :SHARE] = -along_x
    table[PAD : PAD + SHARE, :SHARE] = -along_y
    return split_table(table)


def mode_table():
    k = np.arange(MODES)
    weight = np.where(k == 0, 1.0, 2.0) / math.sqrt(MODES)
    table = np.zeros((8, MODES), np.float32)
    table[0] = weight
    table[1] = weight * 8.0 * k / MODES
    table[2] = (-1.0) ** k - 1.0
    return jnp.asarray(table)


def node_table():
    table = np.zeros((PAD, 128), np.float32)
    table[:SHARE] = np.tile(np.kron(W1, W1), 2)[:, None]
    return jnp.asarray(table)


def device_mode_table():
    k = np.arange(MODES)
    j = np.arange(DISC_LO, DISC_HI)[:, None]
    angle = 2.0 * np.pi / PLANES * ((k[None, :] * j) % PLANES)
    kz = 8.0 * k / MODES
    rows = np.zeros((8, MODES))
    rows[0] = FORWARD * np.cos(angle).sum(axis=0)
    rows[1] = -FORWARD * np.sin(angle).sum(axis=0)
    rows[2] = 1.0 / time_step + viscosity * kz * kz
    table = rows.reshape(8, GROUPS, LOCAL).transpose(1, 0, 2)
    return jnp.asarray(table.astype(np.float32))


def split(value):
    high = value.astype(BF16)
    return high, (value - high.astype(F32)).astype(BF16)


def dot(left, right, transposed=False):
    dims = (((1,), (1 if transposed else 0,)), ((), ()))
    return lax.dot_general(left, right, dims, preferred_element_type=F32)


def dot3(left, right, transposed=False):
    (lh, ll), (rh, rl) = left, right
    return dot(lh, rh, transposed) + (dot(ll, rh, transposed) + dot(lh, rl, transposed))


def planes_kernel(
    width_ref, height_ref, disc_ref, v_ref, ch_ref, cl_ref, sh_ref, sl_ref, gh_ref, gl_ref,
    modes_ref, nodes_ref, out_ref, press_ref,
    ah_ref, al_ref, bh_ref, bl_ref, e_ref, re_ref, im_ref, t0_ref,
):
    me = lax.axis_index("mode")
    zeros = jnp.zeros((PAD - SHARE, 128), F32)
    for c in range(3):
        rows = pl.ds(c * 2 * PAD, 2 * PAD)
        extra = jnp.zeros((2 * PAD, 128), F32)
        for m in range(GROUPS):
            lanes = pl.ds(m * LOCAL, LOCAL)
            re = v_ref[c, pl.ds(m * 2 * SHARE, SHARE, stride=2), :]
            im = v_ref[c, pl.ds(m * 2 * SHARE + 1, SHARE, stride=2), :]
            weight = modes_ref[0:1, lanes]
            wave = modes_ref[1:2, lanes]
            a = jnp.concatenate([re * weight, zeros, im * wave, zeros], axis=0)
            b = jnp.concatenate([im * weight, zeros, re * wave, zeros], axis=0)
            extra = extra + a * modes_ref[2:3, lanes]
            ah_ref[rows, lanes], al_ref[rows, lanes] = split(a)
            bh_ref[rows, lanes], bl_ref[rows, lanes] = split(b)
        e_ref[rows, :] = jnp.broadcast_to(jnp.sum(extra, axis=1, keepdims=True), (2 * PAD, 128))
    re_ref[...] = jnp.zeros_like(re_ref)
    im_ref[...] = jnp.zeros_like(im_ref)
    t0_ref[...] = jnp.zeros_like(t0_ref)
    press_ref[...] = jnp.zeros_like(press_ref)

    row = lax.broadcasted_iota(jnp.int32, (PAD, 1), 0)
    first = row < NN
    width = width_ref[0]
    heights = jnp.where(first, height_ref[2 * me], height_ref[2 * me + 1])
    disc = jnp.where(first, disc_ref[2 * me], disc_ref[2 * me + 1]).astype(F32)
    scale_x = 2.0 / jnp.full((PAD, 1), width)
    scale_y = 2.0 / heights
    press_weight = disc * (width * heights / 4.0) * nodes_ref[:, 0:1]

    def tile_step(t, carry):
        columns = pl.ds(pl.multiple_of(t * TILE, TILE), TILE)
        plane = lax.broadcasted_iota(jnp.int32, (1, TILE), 1) + t * TILE
        start = (plane == 0).astype(F32)
        cos = (ch_ref[:, columns], cl_ref[:, columns])
        sin = (sh_ref[:, columns], sl_ref[:, columns])
        even = dot3((ah_ref[...], al_ref[...]), cos)
        odd = dot3((bh_ref[...], bl_ref[...]), sin)
        fields, along_z = [], []
        for c in range(3):
            base = c * 2 * PAD
            eu, ez = even[base : base + PAD], even[base + PAD : base + 2 * PAD]
            ou, oz = odd[base : base + PAD], odd[base + PAD : base + 2 * PAD]
            fu = e_ref[base : base + PAD, 0:1] * start
            fz = e_ref[base + PAD : base + 2 * PAD, 0:1] * start
            fields.append((eu - ou, eu + ou + fu))
            along_z.append((ez + oz, ez - oz + fz))
        low, high = fields[0]
        in_low = (plane >= DISC_LO).astype(F32)
        in_high = ((plane > PLANES - DISC_HI) | (plane == 0)).astype(F32)
        share = press_weight * (low * low * in_low + high * high * in_high)
        share = jnp.sum(share.reshape(PAD // 8, 8, TILE), axis=0)
        press_ref[...] += share[:, :128] + share[:, 128:]
        gradient = (gh_ref[...], gl_ref[...])
        sums, gaps = [], []
        for c in range(3):
            tends = []
            for side in range(2):
                slopes = dot3(gradient, split(fields[c][side]))
                tends.append(
                    fields[0][side] * scale_x * slopes[:PAD]
                    + fields[1][side] * scale_y * slopes[PAD:]
                    + fields[2][side] * along_z[c][side]
                )
            t0_ref[pl.ds(c * PAD, PAD), :] += (tends[1] * start)[:, :128]
            sums.append(tends[0] + tends[1])
            gaps.append(tends[0] - tends[1])
        re_ref[...] += dot3(split(jnp.concatenate(sums, axis=0)), cos, True)
        im_ref[...] += dot3(split(jnp.concatenate(gaps, axis=0)), sin, True)
        return carry

    lax.fori_loop(0, HALF // TILE, tile_step, 0)
    for c in range(3):
        for m in range(GROUPS):
            lanes = pl.ds(m * LOCAL, LOCAL)
            rows = pl.ds(c * PAD, SHARE)
            re = re_ref[rows, lanes] + t0_ref[rows, 0:1] * modes_ref[2:3, lanes]
            out_ref[c, pl.ds(m * 2 * SHARE, SHARE, stride=2), :] = FORWARD * re
            out_ref[c, pl.ds(m * 2 * SHARE + 1, SHARE, stride=2), :] = -FORWARD * im_ref[rows, lanes]


def row_values(height_ref):
    row = lax.broadcasted_iota(jnp.int32, (ROWS, 128), 0)
    value = jnp.zeros((ROWS, 128), F32)
    for r in range(ROWS):
        value = jnp.where(row == r, height_ref[r].astype(F32), value)
    return value


def next_row(value):
    return jnp.roll(value, -1, axis=0)


def right_kernel(
    width_ref, height_ref, disc_ref, v_ref, t_ref, p0_ref, p1_ref, p2_ref, p3_ref, table_ref,
    b_ref, first_ref, last_ref,
):
    me = lax.axis_index("mode")
    heights = row_values(height_ref)
    disc = row_values(disc_ref)
    width = jnp.full((ROWS, 128), width_ref[0])
    total = jnp.sum(p0_ref[...] + p1_ref[...] + p2_ref[...] + p3_ref[...])
    area = (DISC_HI - DISC_LO) * width * jnp.sum(disc * heights, axis=0, keepdims=True)
    thrust = -(0.5 * thrust_coef * ORDER) * (total / area) / width * disc
    jacobian = width * heights / 4.0
    for c in range(3):
        for p in range(2):
            q = 2 * c + p
            push = thrust * table_ref[me, p : p + 1, :] if c == 0 else None

            def value(a, b):
                at = pl.ds((a * N1 + b) * 2 + p, ROWS, stride=2 * NN)
                node = v_ref[c, at, :] * (1.0 / time_step) + t_ref[c, at, :]
                if push is not None:
                    node = node + push
                return node * (jacobian * (W1[a] * W1[b]))

            for a in range(N1):
                for b in range(1, N1 - 1):
                    b_ref[q, a * N1 + b] = value(a, b)
                upper = value(a, N1 - 1) + next_row(value(a, 0))
                b_ref[q, a * N1 + N1 - 1] = upper
                b_ref[q, a * N1] = jnp.roll(upper, 1, axis=0)
            for b in range(N1 - 1):
                first_ref[q, b] = b_ref[q, b]
                last_ref[q, b] = b_ref[q, (N1 - 1) * N1 + b]


def add_edges(x_ref, before_ref, after_ref, q, store_ref):
    for a in range(1, N1 - 1):
        for b in range(N1):
            store_ref[q, a * N1 + b] = x_ref[q, a * N1 + b]
    for a, edge_ref in ((0, before_ref), (N1 - 1, after_ref)):
        for b in range(N1):
            edge = edge_ref[q, b] if b < N1 - 1 else next_row(edge_ref[q, 0])
            store_ref[q, a * N1 + b] = x_ref[q, a * N1 + b] + edge


def stiff_line(values):
    half = N1 // 2
    even = [values[i] + values[N1 - 1 - i] for i in range(half)] + [values[half]]
    odd = [values[i] - values[N1 - 1 - i] for i in range(half)]
    result = [None] * N1
    for i in range(half + 1):
        total = even[half] * float(K1[i, half])
        for j in range(half):
            total = total + even[j] * float(0.5 * (K1[i, j] + K1[i, N1 - 1 - j]))
        if i == half:
            result[i] = total
        else:
            rest = odd[0] * float(0.5 * (K1[i, 0] - K1[i, N1 - 1]))
            for j in range(1, half):
                rest = rest + odd[j] * float(0.5 * (K1[i, j] - K1[i, N1 - 1 - j]))
            result[i] = total + rest
            result[N1 - 1 - i] = total - rest
    return result


def operator_scales(width_ref, height_ref, table_ref):
    me = lax.axis_index("mode")
    heights = row_values(height_ref)
    width = jnp.full((ROWS, 128), width_ref[0])
    mass = width * heights / 4.0 * table_ref[me, 2:3, :]
    return mass, viscosity * heights / width, viscosity * width / heights


def local_operator(x_ref, q, scratch_ref, scales, emit):
    mass, ratio_x, ratio_y = scales
    for b in range(N1):
        values = [x_ref[q, a * N1 + b] for a in range(N1)]
        for a, stiff in enumerate(stiff_line(values)):
            scratch_ref[a * N1 + b] = mass * values[a] + ratio_x * stiff
    for a in range(N1):
        values = [x_ref[q, a * N1 + b] for b in range(N1)]
        stiff = stiff_line(values)
        emit(
            a,
            values,
            [
                (scratch_ref[a * N1 + b] + ratio_y * stiff[b]) * float(W1[a] * W1[b])
                for b in range(N1)
            ],
        )


def image_kernel(
    width_ref, height_ref, x_ref, before_ref, after_ref, table_ref,
    b_ref, w_ref, first_ref, last_ref, sums_ref, scratch_ref,
):
    scales = operator_scales(width_ref, height_ref, table_ref)

    def part(q, carry):
        add_edges(x_ref, before_ref, after_ref, q, b_ref)
        norm = jnp.zeros((ROWS, 128), F32)
        curve = jnp.zeros((ROWS, 128), F32)
        state = [norm, curve]

        def emit(a, values, image):
            for b in range(N1):
                state[0] = state[0] + values[b] * values[b] * float(MULT[a] * MULT[b])
                state[1] = state[1] + values[b] * image[b]
            upper = image[N1 - 1] + next_row(image[0])
            lower = jnp.roll(upper, 1, axis=0)
            for b in range(N1):
                value = lower if b == 0 else upper if b == N1 - 1 else image[b]
                w_ref[q, a * N1 + b] = value
                if b < N1 - 1 and a == 0:
                    first_ref[q, b] = value
                if b < N1 - 1 and a == N1 - 1:
                    last_ref[q, b] = value

        local_operator(b_ref, q, scratch_ref, scales, emit)
        sums_ref[q, 0] = state[0]
        sums_ref[q, 1] = state[1]
        return carry

    lax.fori_loop(0, 6, part, 0)


def whole(value):
    return jnp.sum(value, axis=0, keepdims=True)


def products_kernel(
    width_ref, height_ref, x_ref, before_ref, after_ref, b_ref, sums_ref, table_ref,
    g_ref, shift_ref, all_ref, scratch_ref,
):
    scales = operator_scales(width_ref, height_ref, table_ref)

    def part(q, carry):
        add_edges(x_ref, before_ref, after_ref, q, g_ref)
        cross = jnp.zeros((ROWS, 128), F32)
        for n in range(NN):
            cross = cross + b_ref[q, n] * g_ref[q, n] * float(MULT[n // N1] * MULT[n % N1])
        norm = whole(sums_ref[q, 0])
        shift = jnp.where(norm > 0, whole(cross) / norm, 0.0)
        for n in range(NN):
            g_ref[q, n] = g_ref[q, n] - shift * b_ref[q, n]
        state = [jnp.zeros((ROWS, 128), F32) for _ in range(3)]

        def emit(a, values, image):
            for b in range(N1):
                state[0] = state[0] + values[b] * values[b] * float(MULT[a] * MULT[b])
                state[1] = state[1] + values[b] * image[b]
                state[2] = state[2] + b_ref[q, a * N1 + b] * image[b]

        local_operator(g_ref, q, scratch_ref, scales, emit)
        rows = [norm, shift, whole(state[0]), whole(state[1]), whole(state[2]), whole(sums_ref[q, 1])]
        block = jnp.concatenate(rows + [jnp.zeros((2, 128), F32)], axis=0)
        shift_ref[q] = block
        for d in range(COLUMNS):
            all_ref[d, q] = block
        return carry

    lax.fori_loop(0, 6, part, 0)


def update_kernel(all_ref, own_ref, b_ref, g_ref, out_ref):
    for c in range(3):
        for p in range(2):
            q = 2 * c + p
            norm = jnp.zeros((1, 128), F32)
            curve = jnp.zeros((1, 128), F32)
            for d in range(COLUMNS):
                norm = norm + all_ref[d, q, 0:1]
                curve = curve + all_ref[d, q, 5:6]
            step = norm / curve
            sigma = curve / norm
            rest = jnp.zeros((1, 128), F32)
            bend = jnp.zeros((1, 128), F32)
            for d in range(COLUMNS):
                gap = all_ref[d, q, 1:2] - sigma
                rest = rest + (all_ref[d, q, 2:3] + gap * gap * all_ref[d, q, 0:1])
                bend = bend + (
                    all_ref[d, q, 3:4] + gap * (2.0 * all_ref[d, q, 4:5] + gap * all_ref[d, q, 5:6])
                )
            norm_next = step * step * rest
            beta = norm_next / norm
            second = norm_next / (step * step * bend - beta * norm_next / step)
            gap = own_ref[q, 1:2] - sigma
            on_b = step + second * (beta - step * gap)
            on_g = -second * step
            for n in range(NN):
                out_ref[c, pl.ds(2 * n + p, ROWS, stride=2 * NN), :] = (
                    on_b * b_ref[q, n] + on_g * g_ref[q, n]
                )


def vmem():
    return pl.BlockSpec(memory_space=pltpu.VMEM)


def smem():
    return pl.BlockSpec(memory_space=pltpu.SMEM)


def call(kernel, specs, outs, scratch, cost, *args):
    return pl.pallas_call(
        kernel,
        in_specs=specs,
        out_specs=[vmem() for _ in outs],
        out_shape=[jax.ShapeDtypeStruct(shape, F32) for shape in outs],
        scratch_shapes=scratch,
        compiler_params=pltpu.CompilerParams(vmem_limit_bytes=VMEM_LIMIT),
        cost_estimate=pl.CostEstimate(flops=int(cost[0]), bytes_accessed=int(cost[1]), transcendentals=0),
    )(*args)


def swap(field):
    blocks = field.reshape(3, GROUPS, SHARE, 2, LOCAL)
    moved = lax.all_to_all(blocks, "mode", split_axis=1, concat_axis=1, tiled=True)
    return moved.reshape(3, 2 * NODES, LOCAL)


def trade(last, first):
    up = [(i, (i + 1) % COLUMNS) for i in range(COLUMNS)]
    down = [(j, i) for i, j in up]
    return lax.ppermute(last, "elem", up), lax.ppermute(first, "elem", down)


def on_device(velocity, column_width, row_height, disc_mask):
    geometry = (column_width, row_height)
    own = velocity.reshape(3, 2 * NODES, LOCAL)
    table = device_mode_table()
    tend, press = call(
        planes_kernel,
        [smem()] * 3 + [vmem()] * 9,
        [(3, 2 * NODES, LOCAL), (8, 128)],
        [pltpu.VMEM((6 * PAD, MODES), BF16) for _ in range(4)]
        + [pltpu.VMEM((6 * PAD, 128), F32)]
        + [pltpu.VMEM((3 * PAD, MODES), F32) for _ in range(2)]
        + [pltpu.VMEM((3 * PAD, 128), F32)],
        (9e9, 8e6),
        *geometry, disc_mask, swap(own), *plane_tables(), *gradient_table(),
        mode_table(), node_table(),
    )
    shares = [press] + [
        lax.ppermute(press, "mode", [(i, (i + d) % GROUPS) for i in range(GROUPS)])
        for d in range(1, GROUPS)
    ]
    field, edge = (6, NN, ROWS, LOCAL), (6, N1 - 1, ROWS, LOCAL)
    part, first, last = call(
        right_kernel,
        [smem()] * 3 + [vmem()] * 7,
        [field, edge, edge],
        [],
        (1e7, 7e6),
        *geometry, disc_mask, own, swap(tend), *shares, table,
    )
    before, after = trade(last, first)
    scratch = [pltpu.VMEM((NN, ROWS, LOCAL), F32)]
    right, part, first, last, sums = call(
        image_kernel,
        [smem()] * 2 + [vmem()] * 4,
        [field, field, edge, edge, (6, 2, ROWS, LOCAL)],
        scratch,
        (3e7, 7e6),
        *geometry, part, before, after, table,
    )
    before, after = trade(last, first)
    gap, blocks, spread = call(
        products_kernel,
        [smem()] * 2 + [vmem()] * 6,
        [field, (6, 8, LOCAL), (COLUMNS, 6, 8, LOCAL)],
        scratch,
        (3e7, 7e6),
        *geometry, part, before, after, right, sums, table,
    )
    everyone = lax.all_to_all(spread, "elem", split_axis=0, concat_axis=0, tiled=True)
    (result,) = call(
        update_kernel,
        [vmem()] * 4,
        [(3, 2 * NODES, LOCAL)],
        [],
        (3e6, 7e6),
        everyone, blocks, right, gap,
    )
    return result.reshape(3, NODES, 2, LOCAL)


def solution(mesh):
    return jax.shard_map(
        on_device,
        mesh=mesh,
        in_specs=(P(None, "elem", None, "mode"), P("elem"), P(), P("elem")),
        out_specs=P(None, "elem", None, "mode"),
        check_vma=False,
    )
```

```python
import functools
import math

import jax
import jax.numpy as jnp
import ml_dtypes
import numpy as np
from jax import lax
from jax.experimental import pallas as pl
from jax.experimental.pallas import tpu as pltpu
from jax.sharding import PartitionSpec as P

ORDER = 8
N1 = ORDER + 1
NN = N1 * N1

gll_points = [
    -1.0,
    -0.8997579954114602,
    -0.6771862795107377,
    -0.3631174638261782,
    0.0,
    0.3631174638261782,
    0.6771862795107377,
    0.8997579954114602,
    1.0,
]
gll_weights = [
    0.0277777777777778,
    0.1654953615608055,
    0.2745387125001617,
    0.3464285109730463,
    0.3715192743764172,
    0.3464285109730463,
    0.2745387125001617,
    0.1654953615608055,
    0.0277777777777778,
]
viscosity = 0.5
time_step = 0.02
thrust_coef = 4.0 / 3.0

MODES = 512
PLANES = 3 * MODES
HALF = PLANES // 2
GROUPS = 4
LOCAL = MODES // GROUPS
ROWS = 8
COLUMNS = 32
NODES = ROWS * NN
SHARE = NODES // GROUPS
ELEM_ROWS = 2 * NN + 2
BLOCK = 2 * ELEM_ROWS
WIDE = BLOCK // 2
SLOT = NN + 1
PAD = 176
TILE = 256
FORWARD = math.sqrt(MODES) / PLANES
DISC_LO = 3 * PLANES // 8
DISC_HI = 5 * PLANES // 8
VMEM_LIMIT = 24 * 1024 * 1024
F32 = jnp.float32
BF16 = jnp.bfloat16


def derivative_matrix():
    points = np.array(gll_points)
    identity = np.eye(9)
    differences = points[:, None] - points[None, :] + identity
    barycentric = 1.0 / np.prod(differences, axis=1)
    off_diagonal = barycentric[None, :] / barycentric[:, None] / differences * (1.0 - identity)
    return off_diagonal - identity * off_diagonal.sum(axis=1)[:, None]


W1 = np.array(gll_weights)
D1 = derivative_matrix()
K1 = (D1.T @ (W1[:, None] * D1)) / W1[:, None]
MULT = np.ones(9)
MULT[0] = MULT[8] = 0.5


def split_table(table):
    table = np.asarray(table, np.float32)
    high = table.astype(ml_dtypes.bfloat16)
    low = (table - high.astype(np.float32)).astype(ml_dtypes.bfloat16)
    return high, low


def plane_tables():
    k = np.arange(MODES)[:, None]
    j = np.arange(HALF)[None, :]
    angle = 2.0 * np.pi / PLANES * ((k * j) % PLANES)
    return [jnp.asarray(t) for t in split_table(np.cos(angle)) + split_table(np.sin(angle))]


def two_elements(matrix):
    table = np.zeros((PAD, PAD))
    for e in range(2):
        at = slice(e * SLOT, e * SLOT + NN)
        table[at, at] = matrix
    return table


def gradient_table():
    one = np.eye(9)
    table = np.concatenate(
        [-two_elements(np.kron(D1, one)), -two_elements(np.kron(one, D1))], axis=0
    )
    return jnp.asarray(np.concatenate(split_table(table), axis=0))


def mode_table():
    k = np.arange(MODES)
    weight = np.where(k == 0, 1.0, 2.0) / math.sqrt(MODES)
    table = np.zeros((8, MODES), np.float32)
    table[0] = weight
    table[1] = weight * 8.0 * k / MODES
    table[2] = (-1.0) ** k - 1.0
    return jnp.asarray(table)


def node_table():
    table = np.zeros((PAD, 128), np.float32)
    for e in range(2):
        table[e * SLOT : e * SLOT + NN] = np.kron(W1, W1)[:, None]
    return jnp.asarray(table)


def device_mode_table():
    k = np.arange(MODES)
    j = np.arange(DISC_LO, DISC_HI)[:, None]
    angle = 2.0 * np.pi / PLANES * ((k[None, :] * j) % PLANES)
    kz = 8.0 * k / MODES
    rows = np.zeros((8, MODES))
    rows[0] = FORWARD * np.cos(angle).sum(axis=0)
    rows[1] = -FORWARD * np.sin(angle).sum(axis=0)
    rows[2] = 1.0 / time_step + viscosity * kz * kz
    table = rows.reshape(8, GROUPS, LOCAL).transpose(1, 0, 2)
    return jnp.asarray(table.astype(np.float32))


def split(value):
    high = value.astype(BF16)
    return jnp.concatenate([high, (value - high.astype(F32)).astype(BF16)], axis=0)


def dot(left, right, transposed=False):
    dims = (((1,), (1 if transposed else 0,)), ((), ()))
    return lax.dot_general(left, right, dims, preferred_element_type=F32)


def dot3(left, right, transposed=False):
    rows = left.shape[0] // 2
    both = dot(left, right[0], transposed)
    return both[:rows] + (both[rows:] + dot(left[:rows], right[1], transposed))


def block_lanes(distance):
    source = lax.rem(lax.axis_index("mode") + GROUPS - distance, GROUPS)
    return pl.ds(pl.multiple_of(source * LOCAL, LOCAL), LOCAL)


def pack_kernel(v_ref, *out_refs):
    me = lax.axis_index("mode")
    for d in range(GROUPS):
        target = lax.rem(me + d, GROUPS)
        for e in range(2):
            out_refs[d][pl.ds(e * ELEM_ROWS, 2 * NN), :] = v_ref[
                0, pl.ds((2 * target + e) * 2 * NN, 2 * NN), :
            ]
            out_refs[d][pl.ds(e * ELEM_ROWS + 2 * NN, 2), :] = jnp.zeros((2, LOCAL), F32)


def plane_tile(t):
    columns = pl.ds(pl.multiple_of(t * TILE, TILE), TILE)
    plane = lax.broadcasted_iota(jnp.int32, (1, TILE), 1) + t * TILE
    return columns, plane


def element_values(ref):
    me = lax.axis_index("mode")
    first = lax.broadcasted_iota(jnp.int32, (PAD, 1), 0) < SLOT
    return jnp.where(first, ref[2 * me].astype(F32), ref[2 * me + 1].astype(F32))


def inverse_kernel(
    with_pressure, width_ref, height_ref, disc_ref, v0_ref, v1_ref, v2_ref, v3_ref,
    ch_ref, cl_ref, sh_ref, sl_ref, modes_ref, nodes_ref, field_ref, along_ref, *rest,
):
    press_ref = rest[0] if with_pressure else None
    a_ref, b_ref = rest[-2:]
    zeros = jnp.zeros((PAD - WIDE, LOCAL), F32)
    extra = jnp.zeros((2 * PAD, LOCAL), F32)
    for d, v_ref in enumerate((v0_ref, v1_ref, v2_ref, v3_ref)):
        lanes = block_lanes(d)
        re = v_ref[pl.ds(0, WIDE, stride=2), :]
        im = v_ref[pl.ds(1, WIDE, stride=2), :]
        weight = modes_ref[0:1, lanes]
        wave = modes_ref[1:2, lanes]
        a = jnp.concatenate([re * weight, zeros, im * wave, zeros], axis=0)
        b = jnp.concatenate([im * weight, zeros, re * wave, zeros], axis=0)
        extra = extra + a * modes_ref[2:3, lanes]
        a_ref[:, lanes] = split(a)
        b_ref[:, lanes] = split(b)
    extra = jnp.sum(extra, axis=1, keepdims=True)
    if with_pressure:
        heights = element_values(height_ref)
        weight = element_values(disc_ref) * (width_ref[0] * heights / 4.0) * nodes_ref[:, 0:1]
        press_ref[...] = jnp.zeros_like(press_ref)
    for t in range(HALF // TILE):
        columns, plane = plane_tile(t)
        even = dot3(a_ref[...], (ch_ref[:, columns], cl_ref[:, columns]))
        odd = dot3(b_ref[...], (sh_ref[:, columns], sl_ref[:, columns]))
        low = even[:PAD] - odd[:PAD]
        high = even[:PAD] + odd[:PAD]
        along_low = even[PAD:] + odd[PAD:]
        along_high = even[PAD:] - odd[PAD:]
        if t == 0:
            start = (plane == 0).astype(F32)
            high = high + extra[:PAD] * start
            along_high = along_high + extra[PAD:] * start
        field_ref[0, :, columns] = low
        field_ref[1, :, columns] = high
        along_ref[0, :, columns] = along_low
        along_ref[1, :, columns] = along_high
        if with_pressure:
            in_low = (plane >= DISC_LO).astype(F32)
            in_high = ((plane > PLANES - DISC_HI) | (plane == 0)).astype(F32)
            share = weight * (low * low * in_low + high * high * in_high)
            share = jnp.sum(share.reshape(PAD // 8, 8, TILE), axis=0)
            press_ref[...] += share[:, :128] + share[:, 128:]


def advection_kernel(
    component, width_ref, height_ref, f0_ref, f1_ref, f2_ref, along_ref,
    ch_ref, cl_ref, sh_ref, sl_ref, gradient_ref, modes_ref, *rest,
):
    press_ref = rest[0] if component == 0 else None
    out_refs = rest[-6:-2]
    re_ref, im_ref = rest[-2:]
    own_ref = (f0_ref, f1_ref, f2_ref)[component]
    scale_x = 2.0 / jnp.full((PAD, 1), width_ref[0])
    scale_y = 2.0 / element_values(height_ref)
    last = None
    for t in range(HALF // TILE):
        columns, plane = plane_tile(t)
        cos = (ch_ref[:, columns], cl_ref[:, columns])
        sin = (sh_ref[:, columns], sl_ref[:, columns])
        tends = []
        for side in range(2):
            field = own_ref[side, :, columns]
            high = field.astype(BF16)
            slopes = dot3(gradient_ref[...], (high, (field - high.astype(F32)).astype(BF16)))
            tends.append(
                f0_ref[side, :, columns] * scale_x * slopes[:PAD]
                + f1_ref[side, :, columns] * scale_y * slopes[PAD:]
                + f2_ref[side, :, columns] * along_ref[side, :, columns]
            )
        re = dot3(split(tends[0] + tends[1]), cos, True)
        im = dot3(split(tends[0] - tends[1]), sin, True)
        if t == 0:
            last = tends[1][:, 0:1]
            re_ref[...] = re + last * modes_ref[2:3, :]
            im_ref[...] = im
        else:
            re_ref[...] += re
            im_ref[...] += im
    for d in range(GROUPS):
        target = lax.rem(lax.axis_index("mode") + d, GROUPS)
        lanes = pl.ds(pl.multiple_of(target * LOCAL, LOCAL), LOCAL)
        out_refs[d][pl.ds(0, WIDE, stride=2), :] = FORWARD * re_ref[pl.ds(0, WIDE), lanes]
        out_refs[d][pl.ds(1, WIDE, stride=2), :] = -FORWARD * im_ref[pl.ds(0, WIDE), lanes]
        if component == 0:
            out_refs[d][pl.ds(2 * NN, 1), :] = jnp.sum(press_ref[...], axis=0, keepdims=True)


def row_values(height_ref):
    row = lax.broadcasted_iota(jnp.int32, (ROWS, 128), 0)
    value = jnp.zeros((ROWS, 128), F32)
    for r in range(ROWS):
        value = jnp.where(row == r, height_ref[r].astype(F32), value)
    return value


def next_row(value):
    return jnp.roll(value, -1, axis=0)


def right_kernel(
    component, width_ref, height_ref, disc_ref, v_ref, t0_ref, t1_ref, t2_ref, t3_ref, table_ref,
    b_ref, first_ref, last_ref, t_ref,
):
    me = lax.axis_index("mode")
    heights = row_values(height_ref)
    width = jnp.full((ROWS, 128), width_ref[0])
    for d, block_ref in enumerate((t0_ref, t1_ref, t2_ref, t3_ref)):
        source = lax.rem(me + GROUPS - d, GROUPS)
        t_ref[pl.ds(pl.multiple_of(source * BLOCK, 8), BLOCK), :] = block_ref[...]
    if component == 0:
        disc = row_values(disc_ref)
        total = sum(ref[2 * NN : 2 * NN + 1, :] for ref in (t0_ref, t1_ref, t2_ref, t3_ref))
        total = jnp.sum(total, axis=1, keepdims=True)
        area = (DISC_HI - DISC_LO) * width * jnp.sum(disc * heights, axis=0, keepdims=True)
        thrust = -(0.5 * thrust_coef * ORDER) * (total / area) / width * disc
    jacobian = width * heights / 4.0
    for p in range(2):
        push = thrust * table_ref[me, p : p + 1, :] if component == 0 else None

        def value(a, b):
            at = (a * N1 + b) * 2 + p
            node = v_ref[0, pl.ds(at, ROWS, stride=2 * NN), :] * (1.0 / time_step)
            node = node + t_ref[pl.ds(at, ROWS, stride=ELEM_ROWS), :]
            if push is not None:
                node = node + push
            return node * (jacobian * float(W1[a] * W1[b]))

        for a in range(N1):
            upper = value(a, N1 - 1) + next_row(value(a, 0))
            lower = jnp.roll(upper, 1, axis=0)
            for b in range(N1):
                node = lower if b == 0 else upper if b == N1 - 1 else value(a, b)
                b_ref[p, a * N1 + b] = node
                if b < N1 - 1 and a == 0:
                    first_ref[p, b] = node
                if b < N1 - 1 and a == N1 - 1:
                    last_ref[p, b] = node


def add_edges(x_ref, before_ref, after_ref, q, store_ref):
    for a in range(1, N1 - 1):
        for b in range(N1):
            store_ref[q, a * N1 + b] = x_ref[q, a * N1 + b]
    for a, edge_ref in ((0, before_ref), (N1 - 1, after_ref)):
        for b in range(N1):
            edge = edge_ref[q, b] if b < N1 - 1 else next_row(edge_ref[q, 0])
            store_ref[q, a * N1 + b] = x_ref[q, a * N1 + b] + edge


def stiff_line(values):
    half = N1 // 2
    even = [values[i] + values[N1 - 1 - i] for i in range(half)] + [values[half]]
    odd = [values[i] - values[N1 - 1 - i] for i in range(half)]
    result = [None] * N1
    for i in range(half + 1):
        total = even[half] * float(K1[i, half])
        for j in range(half):
            total = total + even[j] * float(0.5 * (K1[i, j] + K1[i, N1 - 1 - j]))
        if i == half:
            result[i] = total
        else:
            rest = odd[0] * float(0.5 * (K1[i, 0] - K1[i, N1 - 1]))
            for j in range(1, half):
                rest = rest + odd[j] * float(0.5 * (K1[i, j] - K1[i, N1 - 1 - j]))
            result[i] = total + rest
            result[N1 - 1 - i] = total - rest
    return result


def operator_scales(width_ref, height_ref, table_ref):
    me = lax.axis_index("mode")
    heights = row_values(height_ref)
    width = jnp.full((ROWS, 128), width_ref[0])
    mass = width * heights / 4.0 * table_ref[me, 2:3, :]
    return mass, viscosity * heights / width, viscosity * width / heights


def local_operator(x_ref, q, scratch_ref, scales, emit):
    mass, ratio_x, ratio_y = scales
    for b in range(N1):
        values = [x_ref[q, a * N1 + b] for a in range(N1)]
        for a, stiff in enumerate(stiff_line(values)):
            scratch_ref[a * N1 + b] = mass * values[a] + ratio_x * stiff
    for a in range(N1):
        values = [x_ref[q, a * N1 + b] for b in range(N1)]
        stiff = stiff_line(values)
        emit(
            a,
            values,
            [
                (scratch_ref[a * N1 + b] + ratio_y * stiff[b]) * float(W1[a] * W1[b])
                for b in range(N1)
            ],
        )


def image_kernel(
    width_ref, height_ref, x_ref, before_ref, after_ref, table_ref,
    b_ref, w_ref, first_ref, last_ref, sums_ref, scratch_ref,
):
    scales = operator_scales(width_ref, height_ref, table_ref)

    def part(q, carry):
        add_edges(x_ref, before_ref, after_ref, q, b_ref)
        norm = jnp.zeros((ROWS, 128), F32)
        curve = jnp.zeros((ROWS, 128), F32)
        state = [norm, curve]

        def emit(a, values, image):
            for b in range(N1):
                state[0] = state[0] + values[b] * values[b] * float(MULT[a] * MULT[b])
                state[1] = state[1] + values[b] * image[b]
            upper = image[N1 - 1] + next_row(image[0])
            lower = jnp.roll(upper, 1, axis=0)
            for b in range(N1):
                value = lower if b == 0 else upper if b == N1 - 1 else image[b]
                w_ref[q, a * N1 + b] = value
                if b < N1 - 1 and a == 0:
                    first_ref[q, b] = value
                if b < N1 - 1 and a == N1 - 1:
                    last_ref[q, b] = value

        local_operator(b_ref, q, scratch_ref, scales, emit)
        sums_ref[q, 0] = state[0]
        sums_ref[q, 1] = state[1]
        return carry

    lax.fori_loop(0, 2, part, 0)


def whole(value):
    return jnp.sum(value, axis=0, keepdims=True)


def products_kernel(
    width_ref, height_ref, x_ref, before_ref, after_ref, b_ref, sums_ref, table_ref,
    g_ref, sums_out_ref, scratch_ref,
):
    scales = operator_scales(width_ref, height_ref, table_ref)

    def part(q, carry):
        add_edges(x_ref, before_ref, after_ref, q, g_ref)
        cross = jnp.zeros((ROWS, 128), F32)
        for n in range(NN):
            cross = cross + b_ref[q, n] * g_ref[q, n] * float(MULT[n // N1] * MULT[n % N1])
        norm = whole(sums_ref[q, 0])
        shift = jnp.where(norm > 0, whole(cross) / norm, 0.0)
        for n in range(NN):
            g_ref[q, n] = g_ref[q, n] - shift * b_ref[q, n]
        state = [jnp.zeros((ROWS, 128), F32) for _ in range(3)]

        def emit(a, values, image):
            for b in range(N1):
                state[0] = state[0] + values[b] * values[b] * float(MULT[a] * MULT[b])
                state[1] = state[1] + values[b] * image[b]
                state[2] = state[2] + b_ref[q, a * N1 + b] * image[b]

        local_operator(g_ref, q, scratch_ref, scales, emit)
        rows = [norm, shift, whole(state[0]), whole(state[1]), whole(state[2]), whole(sums_ref[q, 1])]
        block = jnp.concatenate(rows + [jnp.zeros((2, 128), F32)], axis=0)
        sums_out_ref[q] = block
        return carry

    lax.fori_loop(0, 2, part, 0)


def merged(blocks):
    norm = sum(block[0:1] for block in blocks)
    shift = sum(block[0:1] * block[1:2] for block in blocks) / norm
    shift = jnp.where(norm > 0, shift, 0.0)
    rest, bend, mixed = 0.0, 0.0, 0.0
    for block in blocks:
        gap = block[1:2] - shift
        rest = rest + (block[2:3] + gap * gap * block[0:1])
        bend = bend + (block[3:4] + gap * (2.0 * block[4:5] + gap * block[5:6]))
        mixed = mixed + (block[4:5] + gap * block[5:6])
    curve = sum(block[5:6] for block in blocks)
    return norm, shift, rest, bend, mixed, curve


def merge_kernel(*refs):
    *block_refs, out_ref = refs
    for q in range(out_ref.shape[0]):
        rows = merged([ref[q] for ref in block_refs])
        out_ref[q] = jnp.concatenate(list(rows) + [jnp.zeros((2, 128), F32)], axis=0)


def stack_kernel(*refs):
    *block_refs, out_ref = refs
    for c, ref in enumerate(block_refs):
        out_ref[pl.ds(2 * c, 2)] = ref[...]


def update_kernel(own0_ref, own1_ref, own2_ref, s0_ref, s1_ref, s2_ref, s3_ref, *rest):
    *field_refs, out_ref = rest
    for c in range(3):
        own_ref = (own0_ref, own1_ref, own2_ref)[c]
        b_ref, g_ref = field_refs[2 * c : 2 * c + 2]
        for p in range(2):
            q = 2 * c + p
            norm, sigma, rest, bend, _, _ = merged(
                [ref[q] for ref in (s0_ref, s1_ref, s2_ref, s3_ref)]
            )
            step = 1.0 / sigma
            norm_next = step * step * rest
            beta = norm_next / norm
            second = norm_next / (step * step * bend - beta * norm_next / step)
            gap = own_ref[p, 1:2] - sigma
            on_b = step + second * (beta - step * gap)
            on_g = -second * step
            for n in range(NN):
                out_ref[c, pl.ds(2 * n + p, ROWS, stride=2 * NN), :] = (
                    on_b * b_ref[p, n] + on_g * g_ref[p, n]
                )


def vmem():
    return pl.BlockSpec(memory_space=pltpu.VMEM)


def smem():
    return pl.BlockSpec(memory_space=pltpu.SMEM)


def component_block(c):
    return pl.BlockSpec((1, 2 * NODES, LOCAL), lambda i: (c, 0, 0))


class Program:
    def __init__(self):
        self.token = None

    def call(self, kernel, specs, outs, scratch, cost, *args, grid=False):
        def whole_block(shape):
            return pl.BlockSpec(shape, lambda i: (0,) * len(shape)) if grid else vmem()

        if grid:
            specs = [whole_block(a.shape) if s is None else s for s, a in zip(specs, args)]
        else:
            specs = [vmem() if s is None else s for s in specs]
        body, count = kernel, len(args)
        if self.token is not None:
            specs = specs + [pl.BlockSpec(memory_space=pl.ANY)]
            args = args + (self.token,)
            body = lambda *refs: kernel(*refs[:count], *refs[count + 1 :])
        results = pl.pallas_call(
            body,
            grid=(1,) if grid else (),
            in_specs=specs,
            out_specs=[whole_block(shape) for shape in outs],
            out_shape=[jax.ShapeDtypeStruct(shape, F32) for shape in outs],
            scratch_shapes=scratch,
            compiler_params=pltpu.CompilerParams(vmem_limit_bytes=VMEM_LIMIT),
            cost_estimate=pl.CostEstimate(
                flops=int(cost[0]), bytes_accessed=int(cost[1]), transcendentals=0
            ),
        )(*args)
        self.token = results[-1]
        return results


def swap(blocks):
    return [blocks[0]] + [
        lax.ppermute(blocks[d], "mode", [(i, (i + d) % GROUPS) for i in range(GROUPS)])
        for d in range(1, GROUPS)
    ]


def trade(last, first):
    up = [(i, (i + 1) % COLUMNS) for i in range(COLUMNS)]
    down = [(j, i) for i, j in up]
    return lax.ppermute(last, "elem", up), lax.ppermute(first, "elem", down)


def column_pairs(move):
    pairs = []
    for y in range(4):
        for x in range(4):
            for core in range(2):
                y2, x2, core2 = move(y, x, core)
                pairs.append(((y * 4 + x) * 2 + core, ((y2 % 4) * 4 + x2 % 4) * 2 + core2 % 2))
    return pairs


def on_device(velocity, column_width, row_height, disc_mask):
    geometry = (column_width, row_height)
    own = velocity.reshape(3, 2 * NODES, LOCAL)
    table = device_mode_table()
    planes = plane_tables()
    modes = mode_table()
    nodes = node_table()
    gradient = gradient_table()
    block = (BLOCK, LOCAL)
    values = (2, PAD, HALF)
    run = Program()
    sent = [
        swap(
            run.call(
                pack_kernel, [component_block(c)], [block] * GROUPS, [], (1e5, 2e6), own, grid=True
            )
        )
        for c in range(3)
    ]
    fields, alongs, press = [], [], None
    for c in range(3):
        result = run.call(
            functools.partial(inverse_kernel, c == 0),
            [smem()] * 3 + [None] * 10,
            [values, values] + ([(8, 128)] if c == 0 else []),
            [pltpu.VMEM((4 * PAD, MODES), BF16) for _ in range(2)],
            (1.7e9, 6e6),
            *geometry, disc_mask, *sent[c], *planes, modes, nodes,
        )
        fields.append(result[0])
        alongs.append(result[1])
        if c == 0:
            press = result[2]
    returned = [
        swap(
            run.call(
                functools.partial(advection_kernel, c),
                [smem()] * 2 + [None] * (10 + (c == 0)),
                [block] * GROUPS,
                [pltpu.VMEM((PAD, MODES), F32) for _ in range(2)],
                (1.5e9, 8e6),
                *geometry, *fields, alongs[c], *planes, gradient, modes,
                *([press] if c == 0 else []),
            )
        )
        for c in range(3)
    ]
    field, edge = (2, NN, ROWS, LOCAL), (2, N1 - 1, ROWS, LOCAL)
    scratch = [pltpu.VMEM((NN, ROWS, LOCAL), F32)]
    part, rights, gaps, sums, products = {}, {}, {}, {}, {}

    def right(c):
        x, first, last = run.call(
            functools.partial(right_kernel, c),
            [smem()] * 3 + [component_block(c)] + [None] * 5,
            [field, edge, edge],
            [pltpu.VMEM((ROWS * ELEM_ROWS, LOCAL), F32)],
            (1e7, 3e6),
            *geometry, disc_mask, own, *returned[c], table,
            grid=True,
        )
        part[c] = (x, *trade(last, first))

    def image(c):
        rights[c], x, first, last, sums[c] = run.call(
            image_kernel,
            [smem()] * 2 + [None] * 4,
            [field, field, edge, edge, (2, 2, ROWS, LOCAL)],
            scratch,
            (1e7, 3e6),
            *geometry, *part[c], table,
        )
        part[c] = (x, *trade(last, first))

    def product(c):
        gaps[c], products[c] = run.call(
            products_kernel,
            [smem()] * 2 + [None] * 6,
            [field, (2, 8, LOCAL)],
            scratch,
            (1e7, 3e6),
            *geometry, *part[c], rights[c], sums[c], table,
        )

    right(0)
    right(1)
    image(0)
    right(2)
    image(1)
    product(0)
    image(2)
    product(1)
    product(2)
    group = (6, 8, LOCAL)
    own_products = [products[c] for c in range(3)]
    (total,) = run.call(stack_kernel, [None] * 3, [group], [], (1e5, 5e4), *own_products)
    other = lax.ppermute(total, "elem", column_pairs(lambda y, x, core: (y, x, core + 1)))
    (total,) = run.call(merge_kernel, [None] * 2, [group], [], (1e5, 1e5), total, other)
    others = [
        lax.ppermute(total, "elem", column_pairs(lambda y, x, core: (y, x + d, core)))
        for d in range(1, 4)
    ]
    (total,) = run.call(merge_kernel, [None] * 4, [group], [], (1e5, 1e5), total, *others)
    others = [
        lax.ppermute(total, "elem", column_pairs(lambda y, x, core: (y + d, x, core)))
        for d in range(1, 4)
    ]
    (result,) = run.call(
        update_kernel,
        [None] * 13,
        [(3, 2 * NODES, LOCAL)],
        [],
        (3e6, 7e6),
        *own_products, total, *others,
        *[value for c in range(3) for value in (rights[c], gaps[c])],
    )
    return result.reshape(3, NODES, 2, LOCAL)


def solution(mesh):
    return jax.shard_map(
        on_device,
        mesh=mesh,
        in_specs=(P(None, "elem", None, "mode"), P("elem"), P(), P("elem")),
        out_specs=P(None, "elem", None, "mode"),
        check_vma=False,
    )
```

```python
import functools
import math

import jax
import jax.numpy as jnp
import ml_dtypes
import numpy as np
from jax import lax
from jax.experimental import pallas as pl
from jax.experimental.pallas import tpu as pltpu
from jax.sharding import PartitionSpec as P

ORDER = 8
N1 = ORDER + 1
NN = N1 * N1

gll_points = [
    -1.0,
    -0.8997579954114602,
    -0.6771862795107377,
    -0.3631174638261782,
    0.0,
    0.3631174638261782,
    0.6771862795107377,
    0.8997579954114602,
    1.0,
]
gll_weights = [
    0.0277777777777778,
    0.1654953615608055,
    0.2745387125001617,
    0.3464285109730463,
    0.3715192743764172,
    0.3464285109730463,
    0.2745387125001617,
    0.1654953615608055,
    0.0277777777777778,
]
viscosity = 0.5
time_step = 0.02
thrust_coef = 4.0 / 3.0

MODES = 512
PLANES = 3 * MODES
HALF = PLANES // 2
GROUPS = 4
LOCAL = MODES // GROUPS
ROWS = 8
COLUMNS = 32
CHIPS = COLUMNS // 2
NODES = ROWS * NN
SHARE = NODES // GROUPS
ELEM_ROWS = 2 * NN + 2
BLOCK = 2 * ELEM_ROWS
WIDE = BLOCK // 2
SLOT = NN + 1
PAD = 176
TILE = 256
FORWARD = math.sqrt(MODES) / PLANES
DISC_LO = 3 * PLANES // 8
DISC_HI = 5 * PLANES // 8
VMEM_LIMIT = 24 * 1024 * 1024
F32 = jnp.float32
BF16 = jnp.bfloat16


def derivative_matrix():
    points = np.array(gll_points)
    identity = np.eye(9)
    differences = points[:, None] - points[None, :] + identity
    barycentric = 1.0 / np.prod(differences, axis=1)
    off_diagonal = barycentric[None, :] / barycentric[:, None] / differences * (1.0 - identity)
    return off_diagonal - identity * off_diagonal.sum(axis=1)[:, None]


W1 = np.array(gll_weights)
D1 = derivative_matrix()
K1 = (D1.T @ (W1[:, None] * D1)) / W1[:, None]
MULT = np.ones(9)
MULT[0] = MULT[8] = 0.5


def split_table(table):
    table = np.asarray(table, np.float32)
    high = table.astype(ml_dtypes.bfloat16)
    low = (table - high.astype(np.float32)).astype(ml_dtypes.bfloat16)
    return high, low


def plane_tables():
    k = np.arange(MODES)[:, None]
    j = np.arange(HALF)[None, :]
    angle = 2.0 * np.pi / PLANES * ((k * j) % PLANES)
    return [jnp.asarray(t) for t in split_table(np.cos(angle)) + split_table(np.sin(angle))]


def two_elements(matrix):
    table = np.zeros((PAD, PAD))
    for e in range(2):
        at = slice(e * SLOT, e * SLOT + NN)
        table[at, at] = matrix
    return table


def gradient_table():
    one = np.eye(9)
    table = np.concatenate(
        [-two_elements(np.kron(D1, one)), -two_elements(np.kron(one, D1))], axis=0
    )
    return jnp.asarray(np.concatenate(split_table(table), axis=0))


def mode_table():
    k = np.arange(MODES)
    weight = np.where(k == 0, 1.0, 2.0) / math.sqrt(MODES)
    table = np.zeros((8, MODES), np.float32)
    table[0] = weight
    table[1] = weight * 8.0 * k / MODES
    table[2] = (-1.0) ** k - 1.0
    return jnp.asarray(table)


def node_table():
    table = np.zeros((PAD, 128), np.float32)
    for e in range(2):
        table[e * SLOT : e * SLOT + NN] = np.kron(W1, W1)[:, None]
    return jnp.asarray(table)


def device_mode_table():
    k = np.arange(MODES)
    j = np.arange(DISC_LO, DISC_HI)[:, None]
    angle = 2.0 * np.pi / PLANES * ((k[None, :] * j) % PLANES)
    kz = 8.0 * k / MODES
    rows = np.zeros((8, MODES))
    rows[0] = FORWARD * np.cos(angle).sum(axis=0)
    rows[1] = -FORWARD * np.sin(angle).sum(axis=0)
    rows[2] = 1.0 / time_step + viscosity * kz * kz
    table = rows.reshape(8, GROUPS, LOCAL).transpose(1, 0, 2)
    return jnp.asarray(table.astype(np.float32))


def split(value):
    high = value.astype(BF16)
    return jnp.concatenate([high, (value - high.astype(F32)).astype(BF16)], axis=0)


def dot(left, right, transposed=False):
    dims = (((1,), (1 if transposed else 0,)), ((), ()))
    return lax.dot_general(left, right, dims, preferred_element_type=F32)


def dot3(left, right, transposed=False):
    rows = left.shape[0] // 2
    both = dot(left, right[0], transposed)
    return both[:rows] + (both[rows:] + dot(left[:rows], right[1], transposed))


def block_lanes(distance):
    source = lax.rem(lax.axis_index("mode") + GROUPS - distance, GROUPS)
    return pl.ds(pl.multiple_of(source * LOCAL, LOCAL), LOCAL)


def pack_kernel(v_ref, *out_refs):
    me = lax.axis_index("mode")
    for c in range(v_ref.shape[0]):
        for d in range(GROUPS):
            target = lax.rem(me + d, GROUPS)
            for e in range(2):
                base = c * BLOCK + e * ELEM_ROWS
                out_refs[d][pl.ds(base, 2 * NN), :] = v_ref[
                    c, pl.ds((2 * target + e) * 2 * NN, 2 * NN), :
                ]
                out_refs[d][pl.ds(base + 2 * NN, 2), :] = jnp.zeros((2, LOCAL), F32)


def plane_tile(t):
    columns = pl.ds(pl.multiple_of(t * TILE, TILE), TILE)
    plane = lax.broadcasted_iota(jnp.int32, (1, TILE), 1) + t * TILE
    return columns, plane


def element_values(ref):
    me = lax.axis_index("mode")
    first = lax.broadcasted_iota(jnp.int32, (PAD, 1), 0) < SLOT
    return jnp.where(first, ref[2 * me].astype(F32), ref[2 * me + 1].astype(F32))


def load_modes(v_refs, modes_ref, a_ref, b_ref, components):
    zeros = jnp.zeros((PAD - WIDE, LOCAL), F32)
    extra = jnp.zeros((components * 2 * PAD, LOCAL), F32)
    for d, v_ref in enumerate(v_refs):
        lanes = block_lanes(d)
        weight = modes_ref[0:1, lanes]
        wave = modes_ref[1:2, lanes]
        a, b = [], []
        for c in range(components):
            re = v_ref[pl.ds(c * BLOCK, WIDE, stride=2), :]
            im = v_ref[pl.ds(c * BLOCK + 1, WIDE, stride=2), :]
            a += [re * weight, zeros, im * wave, zeros]
            b += [im * weight, zeros, re * wave, zeros]
        a = jnp.concatenate(a, axis=0)
        extra = extra + a * modes_ref[2:3, lanes]
        a_ref[:, lanes] = split(a)
        b_ref[:, lanes] = split(jnp.concatenate(b, axis=0))
    return jnp.sum(extra, axis=1, keepdims=True)


def plane_values(t, a_ref, b_ref, cos, sin, extra):
    _, plane = plane_tile(t)
    even = dot3(a_ref[...], cos)
    odd = dot3(b_ref[...], sin)
    result = []
    for c in range(extra.shape[0] // (2 * PAD)):
        u = slice(2 * c * PAD, (2 * c + 1) * PAD)
        z = slice((2 * c + 1) * PAD, (2 * c + 2) * PAD)
        field = [even[u] - odd[u], even[u] + odd[u]]
        along = [even[z] + odd[z], even[z] - odd[z]]
        if t == 0:
            start = (plane == 0).astype(F32)
            field[1] = field[1] + extra[u] * start
            along[1] = along[1] + extra[z] * start
        result.append((field, along))
    return result


def slope_terms(gradient_ref, field, push_x, push_y):
    high = field.astype(BF16)
    slopes = dot3(gradient_ref[...], (high, (field - high.astype(F32)).astype(BF16)))
    return push_x * slopes[:PAD] + push_y * slopes[PAD:]


def slope_scales(width_ref, height_ref):
    return 2.0 / jnp.full((PAD, 1), width_ref[0]), 2.0 / element_values(height_ref)


def add_modes(t, tends, cos, sin, modes_ref, re_ref, im_ref):
    gather = lambda values: split(jnp.concatenate(values, axis=0))
    re = dot3(gather([low + high for low, high in tends]), cos, True)
    im = dot3(gather([low - high for low, high in tends]), sin, True)
    if t == 0:
        last = jnp.concatenate([high[:, 0:1] for _, high in tends], axis=0)
        re_ref[...] = re + last * modes_ref[2:3, :]
        im_ref[...] = im
    else:
        re_ref[...] += re
        im_ref[...] += im


def store_modes(re_ref, im_ref, out_refs):
    for d in range(GROUPS):
        target = lax.rem(lax.axis_index("mode") + d, GROUPS)
        lanes = pl.ds(pl.multiple_of(target * LOCAL, LOCAL), LOCAL)
        for c in range(re_ref.shape[0] // PAD):
            rows = pl.ds(c * PAD, WIDE)
            out_refs[d][pl.ds(c * BLOCK, WIDE, stride=2), :] = FORWARD * re_ref[rows, lanes]
            out_refs[d][pl.ds(c * BLOCK + 1, WIDE, stride=2), :] = -FORWARD * im_ref[rows, lanes]


def first_kernel(
    width_ref, height_ref, disc_ref, v0_ref, v1_ref, v2_ref, v3_ref,
    ch_ref, cl_ref, sh_ref, sl_ref, gradient_ref, modes_ref, nodes_ref,
    field_ref, along_ref, tend_ref, press_ref, a_ref, b_ref,
):
    extra = load_modes((v0_ref, v1_ref, v2_ref, v3_ref), modes_ref, a_ref, b_ref, 2)
    scale_x, scale_y = slope_scales(width_ref, height_ref)
    heights = element_values(height_ref)
    weight = element_values(disc_ref) * (width_ref[0] * heights / 4.0) * nodes_ref[:, 0:1]
    press_ref[...] = jnp.zeros_like(press_ref)
    for t in range(HALF // TILE):
        columns, plane = plane_tile(t)
        cos = (ch_ref[:, columns], cl_ref[:, columns])
        sin = (sh_ref[:, columns], sl_ref[:, columns])
        values = plane_values(t, a_ref, b_ref, cos, sin, extra)
        for side in range(2):
            push_x = values[0][0][side] * scale_x
            push_y = values[1][0][side] * scale_y
            for c, (field, along) in enumerate(values):
                field_ref[c, side, :, columns] = field[side]
                along_ref[c, side, :, columns] = along[side]
                tend_ref[c, side, :, columns] = slope_terms(
                    gradient_ref, field[side], push_x, push_y
                )
        low, high = values[0][0]
        in_low = (plane >= DISC_LO).astype(F32)
        in_high = ((plane > PLANES - DISC_HI) | (plane == 0)).astype(F32)
        share = weight * (low * low * in_low + high * high * in_high)
        share = jnp.sum(share.reshape(PAD // 8, 8, TILE), axis=0)
        press_ref[...] += share[:, :128] + share[:, 128:]


def second_kernel(
    v0_ref, v1_ref, v2_ref, v3_ref, along01_ref, tend_ref, press_ref,
    ch_ref, cl_ref, sh_ref, sl_ref, modes_ref,
    field_ref, along_ref, o0_ref, o1_ref, o2_ref, o3_ref, a_ref, b_ref, re_ref, im_ref,
):
    out_refs = (o0_ref, o1_ref, o2_ref, o3_ref)
    extra = load_modes((v0_ref, v1_ref, v2_ref, v3_ref), modes_ref, a_ref, b_ref, 1)
    for t in range(HALF // TILE):
        columns, _ = plane_tile(t)
        cos = (ch_ref[:, columns], cl_ref[:, columns])
        sin = (sh_ref[:, columns], sl_ref[:, columns])
        ((field, along),) = plane_values(t, a_ref, b_ref, cos, sin, extra)
        tends = [[None, None], [None, None]]
        for side in range(2):
            field_ref[side, :, columns] = field[side]
            along_ref[side, :, columns] = along[side]
            for c in range(2):
                tends[c][side] = (
                    tend_ref[c, side, :, columns] + field[side] * along01_ref[c, side, :, columns]
                )
        add_modes(t, tends, cos, sin, modes_ref, re_ref, im_ref)
    store_modes(re_ref, im_ref, out_refs)
    for out_ref in out_refs:
        out_ref[pl.ds(2 * NN, 1), :] = jnp.sum(press_ref[...], axis=0, keepdims=True)


def third_kernel(
    width_ref, height_ref, field01_ref, field_ref, along_ref,
    ch_ref, cl_ref, sh_ref, sl_ref, gradient_ref, modes_ref,
    o0_ref, o1_ref, o2_ref, o3_ref, re_ref, im_ref,
):
    scale_x, scale_y = slope_scales(width_ref, height_ref)
    for t in range(HALF // TILE):
        columns, _ = plane_tile(t)
        cos = (ch_ref[:, columns], cl_ref[:, columns])
        sin = (sh_ref[:, columns], sl_ref[:, columns])
        tends = []
        for side in range(2):
            field = field_ref[side, :, columns]
            push_x = field01_ref[0, side, :, columns] * scale_x
            push_y = field01_ref[1, side, :, columns] * scale_y
            tends.append(
                slope_terms(gradient_ref, field, push_x, push_y)
                + field * along_ref[side, :, columns]
            )
        add_modes(t, [tends], cos, sin, modes_ref, re_ref, im_ref)
    store_modes(re_ref, im_ref, (o0_ref, o1_ref, o2_ref, o3_ref))


def row_values(height_ref):
    row = lax.broadcasted_iota(jnp.int32, (ROWS, 128), 0)
    value = jnp.zeros((ROWS, 128), F32)
    for r in range(ROWS):
        value = jnp.where(row == r, height_ref[r].astype(F32), value)
    return value


def next_row(value):
    return jnp.roll(value, -1, axis=0)


def choose_edges(values, inner_ref, outer_ref, at):
    even = lax.rem(lax.axis_index("elem"), 2) == 0
    first, last = values
    inner_ref[at] = jnp.where(even, last, first)
    outer_ref[at] = jnp.where(even, first, last)


def right_kernel(
    thrusted, width_ref, height_ref, disc_ref, v_ref, t0_ref, t1_ref, t2_ref, t3_ref, table_ref,
    b_ref, inner_ref, outer_ref, t_ref,
):
    me = lax.axis_index("mode")
    heights = row_values(height_ref)
    width = jnp.full((ROWS, 128), width_ref[0])
    blocks = (t0_ref, t1_ref, t2_ref, t3_ref)
    if thrusted:
        disc = row_values(disc_ref)
        total = sum(ref[2 * NN : 2 * NN + 1, :] for ref in blocks)
        total = jnp.sum(total, axis=1, keepdims=True)
        area = (DISC_HI - DISC_LO) * width * jnp.sum(disc * heights, axis=0, keepdims=True)
        thrust = -(0.5 * thrust_coef * ORDER) * (total / area) / width * disc
    jacobian = width * heights / 4.0
    for c in range(v_ref.shape[0]):
        for d, block_ref in enumerate(blocks):
            source = lax.rem(me + GROUPS - d, GROUPS)
            rows = pl.ds(pl.multiple_of(source * BLOCK, 8), BLOCK)
            t_ref[c, rows, :] = block_ref[pl.ds(c * BLOCK, BLOCK), :]
    for c in range(v_ref.shape[0]):
        for p in range(2):
            q = 2 * c + p
            push = thrust * table_ref[me, p : p + 1, :] if thrusted and c == 0 else None

            def value(a, b):
                at = (a * N1 + b) * 2 + p
                node = v_ref[c, pl.ds(at, ROWS, stride=2 * NN), :] * (1.0 / time_step)
                node = node + t_ref[c, pl.ds(at, ROWS, stride=ELEM_ROWS), :]
                if push is not None:
                    node = node + push
                return node * (jacobian * float(W1[a] * W1[b]))

            for a in range(N1):
                upper = value(a, N1 - 1) + next_row(value(a, 0))
                lower = jnp.roll(upper, 1, axis=0)
                for b in range(N1):
                    node = lower if b == 0 else upper if b == N1 - 1 else value(a, b)
                    b_ref[q, a * N1 + b] = node
            for b in range(N1 - 1):
                ends = b_ref[q, b], b_ref[q, (N1 - 1) * N1 + b]
                choose_edges(ends, inner_ref, outer_ref, (q, b))


def add_edges(x_ref, inner_ref, outer_ref, q, store_ref):
    even = lax.rem(lax.axis_index("elem"), 2) == 0
    for a in range(1, N1 - 1):
        for b in range(N1):
            store_ref[q, a * N1 + b] = x_ref[q, a * N1 + b]
    for b in range(N1 - 1):
        inner, outer = inner_ref[q, b], outer_ref[q, b]
        for a, edge in ((0, jnp.where(even, outer, inner)), (N1 - 1, jnp.where(even, inner, outer))):
            store_ref[q, a * N1 + b] = x_ref[q, a * N1 + b] + edge
            if b == 0:
                n = a * N1 + N1 - 1
                store_ref[q, n] = x_ref[q, n] + next_row(edge)


def stiff_line(values):
    half = N1 // 2
    even = [values[i] + values[N1 - 1 - i] for i in range(half)] + [values[half]]
    odd = [values[i] - values[N1 - 1 - i] for i in range(half)]
    result = [None] * N1
    for i in range(half + 1):
        total = even[half] * float(K1[i, half])
        for j in range(half):
            total = total + even[j] * float(0.5 * (K1[i, j] + K1[i, N1 - 1 - j]))
        if i == half:
            result[i] = total
        else:
            rest = odd[0] * float(0.5 * (K1[i, 0] - K1[i, N1 - 1]))
            for j in range(1, half):
                rest = rest + odd[j] * float(0.5 * (K1[i, j] - K1[i, N1 - 1 - j]))
            result[i] = total + rest
            result[N1 - 1 - i] = total - rest
    return result


def operator_scales(width_ref, height_ref, table_ref):
    me = lax.axis_index("mode")
    heights = row_values(height_ref)
    width = jnp.full((ROWS, 128), width_ref[0])
    mass = width * heights / 4.0 * table_ref[me, 2:3, :]
    return mass, viscosity * heights / width, viscosity * width / heights


def local_operator(x_ref, q, scratch_ref, scales, emit):
    mass, ratio_x, ratio_y = scales
    for b in range(N1):
        values = [x_ref[q, a * N1 + b] for a in range(N1)]
        for a, stiff in enumerate(stiff_line(values)):
            scratch_ref[a * N1 + b] = mass * values[a] + ratio_x * stiff
    for a in range(N1):
        values = [x_ref[q, a * N1 + b] for b in range(N1)]
        stiff = stiff_line(values)
        emit(
            a,
            values,
            [
                (scratch_ref[a * N1 + b] + ratio_y * stiff[b]) * float(W1[a] * W1[b])
                for b in range(N1)
            ],
        )


def image_kernel(
    width_ref, height_ref, x_ref, from_inner_ref, from_outer_ref, table_ref,
    b_ref, w_ref, inner_ref, outer_ref, sums_ref, scratch_ref,
):
    scales = operator_scales(width_ref, height_ref, table_ref)

    def part(q, carry):
        add_edges(x_ref, from_inner_ref, from_outer_ref, q, b_ref)
        state = [jnp.zeros((ROWS, 128), F32), jnp.zeros((ROWS, 128), F32)]

        def emit(a, values, image):
            for b in range(N1):
                state[0] = state[0] + values[b] * values[b] * float(MULT[a] * MULT[b])
                state[1] = state[1] + values[b] * image[b]
            upper = image[N1 - 1] + next_row(image[0])
            lower = jnp.roll(upper, 1, axis=0)
            for b in range(N1):
                value = lower if b == 0 else upper if b == N1 - 1 else image[b]
                w_ref[q, a * N1 + b] = value

        local_operator(b_ref, q, scratch_ref, scales, emit)
        for b in range(N1 - 1):
            ends = w_ref[q, b], w_ref[q, (N1 - 1) * N1 + b]
            choose_edges(ends, inner_ref, outer_ref, (q, b))
        sums_ref[q, 0] = state[0]
        sums_ref[q, 1] = state[1]
        return carry

    lax.fori_loop(0, x_ref.shape[0], part, 0)


def whole(value):
    return jnp.sum(value, axis=0, keepdims=True)


def products_kernel(
    start, width_ref, height_ref, x_ref, from_inner_ref, from_outer_ref, b_ref, sums_ref, table_ref,
    *rest,
):
    g_ref, out_ref, scratch_ref = rest[-3:]
    scales = operator_scales(width_ref, height_ref, table_ref)
    out_ref[...] = rest[0][...] if start else jnp.zeros_like(out_ref)

    def part(q, carry):
        add_edges(x_ref, from_inner_ref, from_outer_ref, q, g_ref)
        cross = jnp.zeros((ROWS, 128), F32)
        for n in range(NN):
            cross = cross + b_ref[q, n] * g_ref[q, n] * float(MULT[n // N1] * MULT[n % N1])
        norm = whole(sums_ref[q, 0])
        shift = jnp.where(norm > 0, whole(cross) / norm, 0.0)
        for n in range(NN):
            g_ref[q, n] = g_ref[q, n] - shift * b_ref[q, n]
        state = [jnp.zeros((ROWS, 128), F32) for _ in range(3)]

        def emit(a, values, image):
            for b in range(N1):
                state[0] = state[0] + values[b] * values[b] * float(MULT[a] * MULT[b])
                state[1] = state[1] + values[b] * image[b]
                state[2] = state[2] + b_ref[q, a * N1 + b] * image[b]

        local_operator(g_ref, q, scratch_ref, scales, emit)
        rows = [norm, shift] + [whole(value) for value in state] + [whole(sums_ref[q, 1])]
        for i, row in enumerate(rows):
            out_ref[pl.ds(6 * i + start + q, 1), :] = row
        return carry

    lax.fori_loop(0, x_ref.shape[0], part, 0)


def merged(blocks):
    norm = sum(block[0] for block in blocks)
    shift = sum(block[0] * block[1] for block in blocks) / norm
    shift = jnp.where(norm > 0, shift, 0.0)
    rest, bend, mixed = 0.0, 0.0, 0.0
    for block in blocks:
        gap = block[1] - shift
        rest = rest + (block[2] + gap * gap * block[0])
        bend = bend + (block[3] + gap * (2.0 * block[4] + gap * block[5]))
        mixed = mixed + (block[4] + gap * block[5])
    return norm, shift, rest, bend, mixed, sum(block[5] for block in blocks)


def six(read):
    return [read(pl.ds(6 * i, 6)) for i in range(6)]


def merge_kernel(own_ref, other_ref, out_ref):
    rows = merged([six(lambda at: ref[at, :]) for ref in (own_ref, other_ref)])
    rows = jnp.concatenate(list(rows) + [jnp.zeros((4, 128), F32)], axis=0)
    for d in range(CHIPS):
        out_ref[d] = rows


def update_kernel(own_ref, all_ref, b01_ref, g01_ref, b2_ref, g2_ref, out_ref):
    norm, sigma, rest, bend, _, _ = merged(
        [six(lambda at: all_ref[d, at, :]) for d in range(CHIPS)]
    )
    step = 1.0 / sigma
    norm_next = step * step * rest
    beta = norm_next / norm
    second = norm_next / (step * step * bend - beta * norm_next / step)
    gap = own_ref[pl.ds(6, 6), :] - sigma
    on_b = step + second * (beta - step * gap)
    on_g = -second * step
    for c in range(3):
        b_ref, g_ref = (b01_ref, g01_ref) if c < 2 else (b2_ref, g2_ref)
        for p in range(2):
            q = 2 * c + p
            r = q if c < 2 else p
            left, right = on_b[q : q + 1], on_g[q : q + 1]
            for n in range(NN):
                out_ref[c, pl.ds(2 * n + p, ROWS, stride=2 * NN), :] = (
                    left * b_ref[r, n] + right * g_ref[r, n]
                )


def vmem():
    return pl.BlockSpec(memory_space=pltpu.VMEM)


def smem():
    return pl.BlockSpec(memory_space=pltpu.SMEM)


def component_block(start, count):
    return pl.BlockSpec((count, 2 * NODES, LOCAL), lambda i: (start // count, 0, 0))


class Program:
    def __init__(self):
        self.token = None

    def call(self, kernel, specs, outs, scratch, cost, *args, grid=False):
        def whole_block(shape):
            return pl.BlockSpec(shape, lambda i: (0,) * len(shape)) if grid else vmem()

        if grid:
            specs = [whole_block(a.shape) if s is None else s for s, a in zip(specs, args)]
        else:
            specs = [vmem() if s is None else s for s in specs]
        body, count = kernel, len(args)
        if self.token is not None:
            specs = specs + [pl.BlockSpec(memory_space=pl.ANY)]
            args = args + (self.token,)
            body = lambda *refs: kernel(*refs[:count], *refs[count + 1 :])
        results = pl.pallas_call(
            body,
            grid=(1,) if grid else (),
            in_specs=specs,
            out_specs=[whole_block(shape) for shape in outs],
            out_shape=[jax.ShapeDtypeStruct(shape, F32) for shape in outs],
            scratch_shapes=scratch,
            compiler_params=pltpu.CompilerParams(vmem_limit_bytes=VMEM_LIMIT),
            cost_estimate=pl.CostEstimate(
                flops=int(cost[0]), bytes_accessed=int(cost[1]), transcendentals=0
            ),
        )(*args)
        self.token = results[-1]
        return results


def swap(blocks):
    return [blocks[0]] + [
        lax.ppermute(blocks[d], "mode", [(i, (i + d) % GROUPS) for i in range(GROUPS)])
        for d in range(1, GROUPS)
    ]


def trade(inner, outer):
    pair = [(i, i ^ 1) for i in range(COLUMNS)]
    across = [(i, (i + (1 if i % 2 else -1)) % COLUMNS) for i in range(COLUMNS)]
    return lax.ppermute(inner, "elem", pair), lax.ppermute(outer, "elem", across)


def on_device(velocity, column_width, row_height, disc_mask):
    geometry = (column_width, row_height)
    own = velocity.reshape(3, 2 * NODES, LOCAL)
    table = device_mode_table()
    planes = plane_tables()
    modes = mode_table()
    nodes = node_table()
    gradient = gradient_table()
    run = Program()
    chunks = ((0, 2), (2, 1))

    def block(count):
        return (count * BLOCK, LOCAL)

    def values(count):
        return (count, 2, PAD, HALF) if count > 1 else (2, PAD, HALF)

    def rows_scratch(count):
        return [pltpu.VMEM((count * 4 * PAD, MODES), BF16) for _ in range(2)]

    def modes_scratch(count):
        return [pltpu.VMEM((count * PAD, MODES), F32) for _ in range(2)]

    sent = [
        swap(
            run.call(
                pack_kernel, [component_block(*chunk)], [block(chunk[1])] * GROUPS, [], (1e5, 3e6),
                own, grid=True,
            )
        )
        for chunk in chunks
    ]
    field01, along01, tend01, press = run.call(
        first_kernel,
        [smem()] * 3 + [None] * 11,
        [values(2)] * 3 + [(8, 128)],
        rows_scratch(2),
        (4e9, 1e7),
        *geometry, disc_mask, *sent[0], *planes, gradient, modes, nodes,
    )
    field2, along2, *back01 = run.call(
        second_kernel,
        [None] * 12,
        [values(1)] * 2 + [block(2)] * GROUPS,
        rows_scratch(1) + modes_scratch(2),
        (3e9, 1e7),
        *sent[1], along01, tend01, press, *planes, modes,
    )
    back01 = swap(back01)
    back2 = swap(
        run.call(
            third_kernel,
            [smem()] * 2 + [None] * 9,
            [block(1)] * GROUPS,
            modes_scratch(1),
            (2e9, 1e7),
            *geometry, field01, field2, along2, *planes, gradient, modes,
        )
    )
    scratch = [pltpu.VMEM((NN, ROWS, LOCAL), F32)]
    part, rights, gaps, sums = {}, {}, {}, {}

    def field(count):
        return (2 * count, NN, ROWS, LOCAL)

    def edge(count):
        return (2 * count, N1 - 1, ROWS, LOCAL)

    def right(i, back):
        start, count = chunks[i]
        x, *edges = run.call(
            functools.partial(right_kernel, i == 0),
            [smem()] * 3 + [component_block(start, count)] + [None] * 5,
            [field(count), edge(count), edge(count)],
            [pltpu.VMEM((count, ROWS * ELEM_ROWS, LOCAL), F32)],
            (1e7, 3e6),
            *geometry, disc_mask, own, *back, table,
            grid=True,
        )
        part[i] = (x, *trade(*edges))

    def image(i):
        count = chunks[i][1]
        rights[i], x, *edges, sums[i] = run.call(
            image_kernel,
            [smem()] * 2 + [None] * 4,
            [field(count), field(count), edge(count), edge(count), (2 * count, 2, ROWS, LOCAL)],
            scratch,
            (1e7, 3e6),
            *geometry, *part[i], table,
        )
        part[i] = (x, *trade(*edges))

    def product(i, *before):
        start, count = chunks[i]
        gaps[i], total = run.call(
            functools.partial(products_kernel, 2 * start),
            [smem()] * 2 + [None] * (6 + len(before)),
            [field(count), (40, LOCAL)],
            scratch,
            (1e7, 3e6),
            *geometry, *part[i], rights[i], sums[i], table, *before,
        )
        return total

    right(0, back01)
    right(1, back2)
    image(0)
    image(1)
    total = product(0)
    total = product(1, total)
    other = lax.ppermute(total, "elem", [(i, i ^ 1) for i in range(COLUMNS)])
    (spread,) = run.call(
        merge_kernel, [None] * 2, [(CHIPS, 40, LOCAL)], [], (1e5, 1e5), total, other
    )
    everyone = lax.all_to_all(
        spread, "elem", split_axis=0, concat_axis=0, tiled=True,
        axis_index_groups=[[2 * i + core for i in range(CHIPS)] for core in range(2)],
    )
    (result,) = run.call(
        update_kernel,
        [None] * 6,
        [(3, 2 * NODES, LOCAL)],
        [],
        (3e6, 7e6),
        total, everyone, rights[0], gaps[0], rights[1], gaps[1],
    )
    return result.reshape(3, NODES, 2, LOCAL)


def solution(mesh):
    return jax.shard_map(
        on_device,
        mesh=mesh,
        in_specs=(P(None, "elem", None, "mode"), P("elem"), P(), P("elem")),
        out_specs=P(None, "elem", None, "mode"),
        check_vma=False,
    )
```

```python
import functools
import math

import jax
import jax.numpy as jnp
import ml_dtypes
import numpy as np
from jax import lax
from jax.experimental import pallas as pl
from jax.experimental.pallas import tpu as pltpu
from jax.sharding import PartitionSpec as P

ORDER = 8
N1 = ORDER + 1
NN = N1 * N1

gll_points = [
    -1.0,
    -0.8997579954114602,
    -0.6771862795107377,
    -0.3631174638261782,
    0.0,
    0.3631174638261782,
    0.6771862795107377,
    0.8997579954114602,
    1.0,
]
gll_weights = [
    0.0277777777777778,
    0.1654953615608055,
    0.2745387125001617,
    0.3464285109730463,
    0.3715192743764172,
    0.3464285109730463,
    0.2745387125001617,
    0.1654953615608055,
    0.0277777777777778,
]
viscosity = 0.5
time_step = 0.02
thrust_coef = 4.0 / 3.0

MODES = 512
PLANES = 3 * MODES
HALF = PLANES // 2
GROUPS = 4
LOCAL = MODES // GROUPS
ROWS = 8
COLUMNS = 32
CHIPS = COLUMNS // 2
NODES = ROWS * NN
SHARE = NODES // GROUPS
ELEM_ROWS = 2 * NN + 2
BLOCK = 2 * ELEM_ROWS
WIDE = BLOCK // 2
SLOT = NN + 1
PAD = 176
TILE = 256
FORWARD = math.sqrt(MODES) / PLANES
DISC_LO = 3 * PLANES // 8
DISC_HI = 5 * PLANES // 8
VMEM_LIMIT = 24 * 1024 * 1024
F32 = jnp.float32
BF16 = jnp.bfloat16


def derivative_matrix():
    points = np.array(gll_points)
    identity = np.eye(9)
    differences = points[:, None] - points[None, :] + identity
    barycentric = 1.0 / np.prod(differences, axis=1)
    off_diagonal = barycentric[None, :] / barycentric[:, None] / differences * (1.0 - identity)
    return off_diagonal - identity * off_diagonal.sum(axis=1)[:, None]


W1 = np.array(gll_weights)
D1 = derivative_matrix()
K1 = (D1.T @ (W1[:, None] * D1)) / W1[:, None]
MULT = np.ones(9)
MULT[0] = MULT[8] = 0.5


def split_table(table):
    table = np.asarray(table, np.float32)
    high = table.astype(ml_dtypes.bfloat16)
    low = (table - high.astype(np.float32)).astype(ml_dtypes.bfloat16)
    return high, low


def plane_tables():
    k = np.arange(MODES)[:, None]
    j = np.arange(HALF)[None, :]
    angle = 2.0 * np.pi / PLANES * ((k * j) % PLANES)
    return [jnp.asarray(t) for t in split_table(np.cos(angle)) + split_table(np.sin(angle))]


def two_elements(matrix):
    table = np.zeros((PAD, PAD))
    for e in range(2):
        at = slice(e * SLOT, e * SLOT + NN)
        table[at, at] = matrix
    return table


def gradient_table():
    one = np.eye(9)
    table = np.concatenate(
        [-two_elements(np.kron(D1, one)), -two_elements(np.kron(one, D1))], axis=0
    )
    return jnp.asarray(np.concatenate(split_table(table), axis=0))


def mode_table():
    k = np.arange(MODES)
    weight = np.where(k == 0, 1.0, 2.0) / math.sqrt(MODES)
    table = np.zeros((8, MODES), np.float32)
    table[0] = weight
    table[1] = weight * 8.0 * k / MODES
    table[2] = (-1.0) ** k - 1.0
    return jnp.asarray(table)


def node_table():
    table = np.zeros((PAD, 128), np.float32)
    for e in range(2):
        table[e * SLOT : e * SLOT + NN] = np.kron(W1, W1)[:, None]
    return jnp.asarray(table)


def device_mode_table():
    k = np.arange(MODES)
    j = np.arange(DISC_LO, DISC_HI)[:, None]
    angle = 2.0 * np.pi / PLANES * ((k[None, :] * j) % PLANES)
    kz = 8.0 * k / MODES
    rows = np.zeros((8, MODES))
    rows[0] = FORWARD * np.cos(angle).sum(axis=0)
    rows[1] = -FORWARD * np.sin(angle).sum(axis=0)
    rows[2] = 1.0 / time_step + viscosity * kz * kz
    table = rows.reshape(8, GROUPS, LOCAL).transpose(1, 0, 2)
    return jnp.asarray(table.astype(np.float32))


def split(value):
    high = value.astype(BF16)
    return jnp.concatenate([high, (value - high.astype(F32)).astype(BF16)], axis=0)


def dot(left, right, transposed=False):
    dims = (((1,), (1 if transposed else 0,)), ((), ()))
    return lax.dot_general(left, right, dims, preferred_element_type=F32)


def dot3(left, right, transposed=False):
    rows = left.shape[0] // 2
    both = dot(left, right[0], transposed)
    return both[:rows] + (both[rows:] + dot(left[:rows], right[1], transposed))


def block_lanes(distance):
    source = lax.rem(lax.axis_index("mode") + GROUPS - distance, GROUPS)
    return pl.ds(pl.multiple_of(source * LOCAL, LOCAL), LOCAL)


def pack_kernel(v_ref, *out_refs):
    me = lax.axis_index("mode")
    for c in range(v_ref.shape[0]):
        for d in range(GROUPS):
            target = lax.rem(me + d, GROUPS)
            for e in range(2):
                base = c * BLOCK + e * ELEM_ROWS
                out_refs[d][pl.ds(base, 2 * NN), :] = v_ref[
                    c, pl.ds((2 * target + e) * 2 * NN, 2 * NN), :
                ]
                out_refs[d][pl.ds(base + 2 * NN, 2), :] = jnp.zeros((2, LOCAL), F32)


def plane_tile(t):
    columns = pl.ds(pl.multiple_of(t * TILE, TILE), TILE)
    plane = lax.broadcasted_iota(jnp.int32, (1, TILE), 1) + t * TILE
    return columns, plane


def element_values(ref):
    me = lax.axis_index("mode")
    first = lax.broadcasted_iota(jnp.int32, (PAD, 1), 0) < SLOT
    return jnp.where(first, ref[2 * me].astype(F32), ref[2 * me + 1].astype(F32))


def load_modes(v_refs, modes_ref, a_ref, b_ref, components):
    zeros = jnp.zeros((PAD - WIDE, LOCAL), F32)
    extra = jnp.zeros((components * 2 * PAD, LOCAL), F32)
    for d, v_ref in enumerate(v_refs):
        lanes = block_lanes(d)
        weight = modes_ref[0:1, lanes]
        wave = modes_ref[1:2, lanes]
        a, b = [], []
        for c in range(components):
            re = v_ref[pl.ds(c * BLOCK, WIDE, stride=2), :]
            im = v_ref[pl.ds(c * BLOCK + 1, WIDE, stride=2), :]
            a += [re * weight, zeros, im * wave, zeros]
            b += [im * weight, zeros, re * wave, zeros]
        a = jnp.concatenate(a, axis=0)
        extra = extra + a * modes_ref[2:3, lanes]
        a_ref[:, lanes] = split(a)
        b_ref[:, lanes] = split(jnp.concatenate(b, axis=0))
    return jnp.sum(extra, axis=1, keepdims=True)


def plane_values(t, a_ref, b_ref, cos, sin, extra):
    _, plane = plane_tile(t)
    even = dot3(a_ref[...], cos)
    odd = dot3(b_ref[...], sin)
    result = []
    for c in range(extra.shape[0] // (2 * PAD)):
        u = slice(2 * c * PAD, (2 * c + 1) * PAD)
        z = slice((2 * c + 1) * PAD, (2 * c + 2) * PAD)
        field = [even[u] - odd[u], even[u] + odd[u]]
        along = [even[z] + odd[z], even[z] - odd[z]]
        if t == 0:
            start = (plane == 0).astype(F32)
            field[1] = field[1] + extra[u] * start
            along[1] = along[1] + extra[z] * start
        result.append((field, along))
    return result


def slope_terms(gradient_ref, field, push_x, push_y):
    high = field.astype(BF16)
    slopes = dot3(gradient_ref[...], (high, (field - high.astype(F32)).astype(BF16)))
    return push_x * slopes[:PAD] + push_y * slopes[PAD:]


def slope_scales(width_ref, height_ref):
    return 2.0 / jnp.full((PAD, 1), width_ref[0]), 2.0 / element_values(height_ref)


def add_modes(t, tends, cos, sin, modes_ref, re_ref, im_ref):
    gather = lambda values: split(jnp.concatenate(values, axis=0))
    re = dot3(gather([low + high for low, high in tends]), cos, True)
    im = dot3(gather([low - high for low, high in tends]), sin, True)
    if t == 0:
        last = jnp.concatenate([high[:, 0:1] for _, high in tends], axis=0)
        re_ref[...] = re + last * modes_ref[2:3, :]
        im_ref[...] = im
    else:
        re_ref[...] += re
        im_ref[...] += im


def store_modes(re_ref, im_ref, out_refs):
    for d in range(GROUPS):
        target = lax.rem(lax.axis_index("mode") + d, GROUPS)
        lanes = pl.ds(pl.multiple_of(target * LOCAL, LOCAL), LOCAL)
        for c in range(re_ref.shape[0] // PAD):
            rows = pl.ds(c * PAD, WIDE)
            out_refs[d][pl.ds(c * BLOCK, WIDE, stride=2), :] = FORWARD * re_ref[rows, lanes]
            out_refs[d][pl.ds(c * BLOCK + 1, WIDE, stride=2), :] = -FORWARD * im_ref[rows, lanes]


def first_kernel(
    width_ref, height_ref, disc_ref, v0_ref, v1_ref, v2_ref, v3_ref,
    ch_ref, cl_ref, sh_ref, sl_ref, gradient_ref, modes_ref, nodes_ref,
    field_ref, along_ref, tend_ref, press_ref, a_ref, b_ref,
):
    extra = load_modes((v0_ref, v1_ref, v2_ref, v3_ref), modes_ref, a_ref, b_ref, 2)
    scale_x, scale_y = slope_scales(width_ref, height_ref)
    heights = element_values(height_ref)
    weight = element_values(disc_ref) * (width_ref[0] * heights / 4.0) * nodes_ref[:, 0:1]
    press_ref[...] = jnp.zeros_like(press_ref)
    for t in range(HALF // TILE):
        columns, plane = plane_tile(t)
        cos = (ch_ref[:, columns], cl_ref[:, columns])
        sin = (sh_ref[:, columns], sl_ref[:, columns])
        values = plane_values(t, a_ref, b_ref, cos, sin, extra)
        for side in range(2):
            push_x = values[0][0][side] * scale_x
            push_y = values[1][0][side] * scale_y
            for c, (field, along) in enumerate(values):
                field_ref[c, side, :, columns] = field[side]
                along_ref[c, side, :, columns] = along[side]
                tend_ref[c, side, :, columns] = slope_terms(
                    gradient_ref, field[side], push_x, push_y
                )
        low, high = values[0][0]
        in_low = (plane >= DISC_LO).astype(F32)
        in_high = ((plane > PLANES - DISC_HI) | (plane == 0)).astype(F32)
        share = weight * (low * low * in_low + high * high * in_high)
        share = jnp.sum(share.reshape(PAD // 8, 8, TILE), axis=0)
        press_ref[...] += share[:, :128] + share[:, 128:]


def second_kernel(
    v0_ref, v1_ref, v2_ref, v3_ref, along01_ref, tend_ref, press_ref,
    ch_ref, cl_ref, sh_ref, sl_ref, modes_ref,
    field_ref, along_ref, o0_ref, o1_ref, o2_ref, o3_ref, a_ref, b_ref, re_ref, im_ref,
):
    out_refs = (o0_ref, o1_ref, o2_ref, o3_ref)
    extra = load_modes((v0_ref, v1_ref, v2_ref, v3_ref), modes_ref, a_ref, b_ref, 1)
    for t in range(HALF // TILE):
        columns, _ = plane_tile(t)
        cos = (ch_ref[:, columns], cl_ref[:, columns])
        sin = (sh_ref[:, columns], sl_ref[:, columns])
        ((field, along),) = plane_values(t, a_ref, b_ref, cos, sin, extra)
        tends = [[None, None], [None, None]]
        for side in range(2):
            field_ref[side, :, columns] = field[side]
            along_ref[side, :, columns] = along[side]
            for c in range(2):
                tends[c][side] = (
                    tend_ref[c, side, :, columns] + field[side] * along01_ref[c, side, :, columns]
                )
        add_modes(t, tends, cos, sin, modes_ref, re_ref, im_ref)
    store_modes(re_ref, im_ref, out_refs)
    for out_ref in out_refs:
        out_ref[pl.ds(2 * NN, 1), :] = jnp.sum(press_ref[...], axis=0, keepdims=True)


def choose_edges(values, inner_ref, outer_ref, at):
    even = lax.rem(lax.axis_index("elem"), 2) == 0
    first, last = values
    inner_ref[at] = jnp.where(even, last, first)
    outer_ref[at] = jnp.where(even, first, last)


def edge_rows(side, part, element):
    return pl.ds((2 * part + element) * N1, N1), element * SLOT + side * (NN - N1)


def third_kernel(
    width_ref, height_ref, field01_ref, field_ref, along_ref, v0_ref, v1_ref, v2_ref, v3_ref,
    ch_ref, cl_ref, sh_ref, sl_ref, gradient_ref, modes_ref,
    re_ref, im_ref, inner_ref, outer_ref, first_ref, last_ref,
):
    scale_x, scale_y = slope_scales(width_ref, height_ref)
    for t in range(HALF // TILE):
        columns, _ = plane_tile(t)
        cos = (ch_ref[:, columns], cl_ref[:, columns])
        sin = (sh_ref[:, columns], sl_ref[:, columns])
        tends = []
        for side in range(2):
            field = field_ref[side, :, columns]
            push_x = field01_ref[0, side, :, columns] * scale_x
            push_y = field01_ref[1, side, :, columns] * scale_y
            tends.append(
                slope_terms(gradient_ref, field, push_x, push_y)
                + field * along_ref[side, :, columns]
            )
        add_modes(t, [tends], cos, sin, modes_ref, re_ref, im_ref)
    for side, edge_ref in enumerate((first_ref, last_ref)):
        edge_ref[...] = jnp.zeros_like(edge_ref)
        for p in range(2):
            for e in range(2):
                rows, start = edge_rows(side, p, e)
                for d, v_ref in enumerate((v0_ref, v1_ref, v2_ref, v3_ref)):
                    edge_ref[rows, block_lanes(d)] = v_ref[pl.ds(2 * start + p, N1, stride=2), :]
                tend = FORWARD * re_ref[pl.ds(start, N1), :] if p == 0 else (
                    -FORWARD * im_ref[pl.ds(start, N1), :]
                )
                edge_ref[rows, :] = (edge_ref[rows, :] * (1.0 / time_step) + tend) * width_ref[0]
    choose_edges((first_ref[...], last_ref[...]), inner_ref, outer_ref, ...)


def fourth_kernel(
    width_ref, re_ref, im_ref, from_inner_ref, from_outer_ref,
    o0_ref, o1_ref, o2_ref, o3_ref, re_sum_ref, im_sum_ref,
):
    even = lax.rem(lax.axis_index("elem"), 2) == 0
    re_sum_ref[...] = re_ref[...]
    im_sum_ref[...] = im_ref[...]
    scale = 1.0 / (FORWARD * jnp.full((N1, MODES), width_ref[0]))
    for side in range(2):
        for p in range(2):
            for e in range(2):
                rows, start = edge_rows(side, p, e)
                inner, outer = from_inner_ref[rows, :], from_outer_ref[rows, :]
                edge = jnp.where(even, inner, outer) if side else jnp.where(even, outer, inner)
                if p == 0:
                    re_sum_ref[pl.ds(start, N1), :] += edge * scale
                else:
                    im_sum_ref[pl.ds(start, N1), :] -= edge * scale
    store_modes(re_sum_ref, im_sum_ref, (o0_ref, o1_ref, o2_ref, o3_ref))


def row_values(height_ref):
    row = lax.broadcasted_iota(jnp.int32, (ROWS, 128), 0)
    value = jnp.zeros((ROWS, 128), F32)
    for r in range(ROWS):
        value = jnp.where(row == r, height_ref[r].astype(F32), value)
    return value


def next_row(value):
    return jnp.roll(value, -1, axis=0)


def right_side(thrusted, width_ref, height_ref, disc_ref, v_ref, blocks, table_ref, b_ref, t_ref):
    me = lax.axis_index("mode")
    heights = row_values(height_ref)
    width = jnp.full((ROWS, 128), width_ref[0])
    if thrusted:
        disc = row_values(disc_ref)
        total = sum(ref[2 * NN : 2 * NN + 1, :] for ref in blocks)
        total = jnp.sum(total, axis=1, keepdims=True)
        area = (DISC_HI - DISC_LO) * width * jnp.sum(disc * heights, axis=0, keepdims=True)
        thrust = -(0.5 * thrust_coef * ORDER) * (total / area) / width * disc
    jacobian = width * heights / 4.0
    for c in range(v_ref.shape[0]):
        for d, block_ref in enumerate(blocks):
            source = lax.rem(me + GROUPS - d, GROUPS)
            rows = pl.ds(pl.multiple_of(source * BLOCK, 8), BLOCK)
            t_ref[c, rows, :] = block_ref[pl.ds(c * BLOCK, BLOCK), :]
    for c in range(v_ref.shape[0]):
        for p in range(2):
            q = 2 * c + p
            push = thrust * table_ref[me, p : p + 1, :] if thrusted and c == 0 else None

            def value(a, b):
                at = (a * N1 + b) * 2 + p
                node = v_ref[c, pl.ds(at, ROWS, stride=2 * NN), :] * (1.0 / time_step)
                node = node + t_ref[c, pl.ds(at, ROWS, stride=ELEM_ROWS), :]
                if push is not None:
                    node = node + push
                return node * (jacobian * float(W1[a] * W1[b]))

            for a in range(N1):
                upper = value(a, N1 - 1) + next_row(value(a, 0))
                lower = jnp.roll(upper, 1, axis=0)
                for b in range(N1):
                    node = lower if b == 0 else upper if b == N1 - 1 else value(a, b)
                    b_ref[q, a * N1 + b] = node


def choose_all_edges(x_ref, inner_ref, outer_ref, q):
    for b in range(N1 - 1):
        ends = x_ref[q, b], x_ref[q, (N1 - 1) * N1 + b]
        choose_edges(ends, inner_ref, outer_ref, (q, b))


def right_kernel(
    width_ref, height_ref, disc_ref, v_ref, t0_ref, t1_ref, t2_ref, t3_ref, table_ref,
    b_ref, inner_ref, outer_ref, t_ref,
):
    blocks = (t0_ref, t1_ref, t2_ref, t3_ref)
    right_side(True, width_ref, height_ref, disc_ref, v_ref, blocks, table_ref, b_ref, t_ref)
    for q in range(b_ref.shape[0]):
        choose_all_edges(b_ref, inner_ref, outer_ref, q)


def add_edges(x_ref, inner_ref, outer_ref, q, store_ref):
    even = lax.rem(lax.axis_index("elem"), 2) == 0
    for a in range(1, N1 - 1):
        for b in range(N1):
            store_ref[q, a * N1 + b] = x_ref[q, a * N1 + b]
    for b in range(N1 - 1):
        inner, outer = inner_ref[q, b], outer_ref[q, b]
        for a, edge in ((0, jnp.where(even, outer, inner)), (N1 - 1, jnp.where(even, inner, outer))):
            store_ref[q, a * N1 + b] = x_ref[q, a * N1 + b] + edge
            if b == 0:
                n = a * N1 + N1 - 1
                store_ref[q, n] = x_ref[q, n] + next_row(edge)


def stiff_line(values):
    half = N1 // 2
    even = [values[i] + values[N1 - 1 - i] for i in range(half)] + [values[half]]
    odd = [values[i] - values[N1 - 1 - i] for i in range(half)]
    result = [None] * N1
    for i in range(half + 1):
        total = even[half] * float(K1[i, half])
        for j in range(half):
            total = total + even[j] * float(0.5 * (K1[i, j] + K1[i, N1 - 1 - j]))
        if i == half:
            result[i] = total
        else:
            rest = odd[0] * float(0.5 * (K1[i, 0] - K1[i, N1 - 1]))
            for j in range(1, half):
                rest = rest + odd[j] * float(0.5 * (K1[i, j] - K1[i, N1 - 1 - j]))
            result[i] = total + rest
            result[N1 - 1 - i] = total - rest
    return result


def operator_scales(width_ref, height_ref, table_ref):
    me = lax.axis_index("mode")
    heights = row_values(height_ref)
    width = jnp.full((ROWS, 128), width_ref[0])
    mass = width * heights / 4.0 * table_ref[me, 2:3, :]
    return mass, viscosity * heights / width, viscosity * width / heights


def local_operator(x_ref, q, scratch_ref, scales, emit):
    mass, ratio_x, ratio_y = scales
    for b in range(N1):
        values = [x_ref[q, a * N1 + b] for a in range(N1)]
        for a, stiff in enumerate(stiff_line(values)):
            scratch_ref[a * N1 + b] = mass * values[a] + ratio_x * stiff
    for a in range(N1):
        values = [x_ref[q, a * N1 + b] for b in range(N1)]
        stiff = stiff_line(values)
        emit(
            a,
            values,
            [
                (scratch_ref[a * N1 + b] + ratio_y * stiff[b]) * float(W1[a] * W1[b])
                for b in range(N1)
            ],
        )


def image_side(scales, b_ref, w_ref, inner_ref, outer_ref, sums_ref, scratch_ref, q):
    state = [jnp.zeros((ROWS, 128), F32), jnp.zeros((ROWS, 128), F32)]

    def emit(a, values, image):
        for b in range(N1):
            state[0] = state[0] + values[b] * values[b] * float(MULT[a] * MULT[b])
            state[1] = state[1] + values[b] * image[b]
        upper = image[N1 - 1] + next_row(image[0])
        lower = jnp.roll(upper, 1, axis=0)
        for b in range(N1):
            value = lower if b == 0 else upper if b == N1 - 1 else image[b]
            w_ref[q, a * N1 + b] = value

    local_operator(b_ref, q, scratch_ref, scales, emit)
    choose_all_edges(w_ref, inner_ref, outer_ref, q)
    sums_ref[q, 0] = state[0]
    sums_ref[q, 1] = state[1]


def image_kernel(
    width_ref, height_ref, x_ref, from_inner_ref, from_outer_ref, table_ref,
    b_ref, w_ref, inner_ref, outer_ref, sums_ref, scratch_ref,
):
    scales = operator_scales(width_ref, height_ref, table_ref)

    def part(q, carry):
        add_edges(x_ref, from_inner_ref, from_outer_ref, q, b_ref)
        image_side(scales, b_ref, w_ref, inner_ref, outer_ref, sums_ref, scratch_ref, q)
        return carry

    lax.fori_loop(0, x_ref.shape[0], part, 0)


def right_image_kernel(
    width_ref, height_ref, v_ref, t0_ref, t1_ref, t2_ref, t3_ref, table_ref,
    b_ref, w_ref, inner_ref, outer_ref, sums_ref, t_ref, scratch_ref,
):
    blocks = (t0_ref, t1_ref, t2_ref, t3_ref)
    right_side(False, width_ref, height_ref, None, v_ref, blocks, table_ref, b_ref, t_ref)
    scales = operator_scales(width_ref, height_ref, table_ref)

    def part(q, carry):
        image_side(scales, b_ref, w_ref, inner_ref, outer_ref, sums_ref, scratch_ref, q)
        return carry

    lax.fori_loop(0, b_ref.shape[0], part, 0)


def whole(value):
    return jnp.sum(value, axis=0, keepdims=True)


def products_kernel(
    start, chained, width_ref, height_ref, x_ref, from_inner_ref, from_outer_ref, b_ref, sums_ref, table_ref,
    *rest,
):
    g_ref, out_ref, scratch_ref = rest[-3:]
    scales = operator_scales(width_ref, height_ref, table_ref)
    out_ref[...] = rest[0][...] if chained else jnp.zeros_like(out_ref)

    def part(q, carry):
        add_edges(x_ref, from_inner_ref, from_outer_ref, q, g_ref)
        cross = jnp.zeros((ROWS, 128), F32)
        for n in range(NN):
            cross = cross + b_ref[q, n] * g_ref[q, n] * float(MULT[n // N1] * MULT[n % N1])
        norm = whole(sums_ref[q, 0])
        shift = jnp.where(norm > 0, whole(cross) / norm, 0.0)
        for n in range(NN):
            g_ref[q, n] = g_ref[q, n] - shift * b_ref[q, n]
        state = [jnp.zeros((ROWS, 128), F32) for _ in range(3)]

        def emit(a, values, image):
            for b in range(N1):
                state[0] = state[0] + values[b] * values[b] * float(MULT[a] * MULT[b])
                state[1] = state[1] + values[b] * image[b]
                state[2] = state[2] + b_ref[q, a * N1 + b] * image[b]

        local_operator(g_ref, q, scratch_ref, scales, emit)
        rows = [norm, shift] + [whole(value) for value in state] + [whole(sums_ref[q, 1])]
        for i, row in enumerate(rows):
            out_ref[pl.ds(6 * i + start + q, 1), :] = row
        return carry

    lax.fori_loop(0, x_ref.shape[0], part, 0)


def merged(blocks):
    norm = sum(block[0] for block in blocks)
    shift = sum(block[0] * block[1] for block in blocks) / norm
    shift = jnp.where(norm > 0, shift, 0.0)
    rest, bend, mixed = 0.0, 0.0, 0.0
    for block in blocks:
        gap = block[1] - shift
        rest = rest + (block[2] + gap * gap * block[0])
        bend = bend + (block[3] + gap * (2.0 * block[4] + gap * block[5]))
        mixed = mixed + (block[4] + gap * block[5])
    return norm, shift, rest, bend, mixed, sum(block[5] for block in blocks)


def six(read):
    return [read(pl.ds(6 * i, 6)) for i in range(6)]


def merge_kernel(own_ref, other_ref, out_ref):
    rows = merged([six(lambda at: ref[at, :]) for ref in (own_ref, other_ref)])
    rows = jnp.concatenate(list(rows) + [jnp.zeros((4, 128), F32)], axis=0)
    for d in range(CHIPS):
        out_ref[d] = rows


def update_kernel(own_ref, all_ref, b01_ref, g01_ref, b2_ref, g2_ref, out_ref):
    norm, sigma, rest, bend, _, _ = merged(
        [six(lambda at: all_ref[d, at, :]) for d in range(CHIPS)]
    )
    step = 1.0 / sigma
    norm_next = step * step * rest
    beta = norm_next / norm
    second = norm_next / (step * step * bend - beta * norm_next / step)
    gap = own_ref[pl.ds(6, 6), :] - sigma
    on_b = step + second * (beta - step * gap)
    on_g = -second * step
    for c in range(3):
        b_ref, g_ref = (b01_ref, g01_ref) if c < 2 else (b2_ref, g2_ref)
        for p in range(2):
            q = 2 * c + p
            r = q if c < 2 else p
            left, right = on_b[q : q + 1], on_g[q : q + 1]
            for n in range(NN):
                out_ref[c, pl.ds(2 * n + p, ROWS, stride=2 * NN), :] = (
                    left * b_ref[r, n] + right * g_ref[r, n]
                )


def vmem():
    return pl.BlockSpec(memory_space=pltpu.VMEM)


def smem():
    return pl.BlockSpec(memory_space=pltpu.SMEM)


def component_block(start, count):
    return pl.BlockSpec((count, 2 * NODES, LOCAL), lambda i: (start // count, 0, 0))


class Program:
    def __init__(self):
        self.token = None

    def call(self, kernel, specs, outs, scratch, cost, *args, grid=False, after=()):
        def whole_block(shape):
            return pl.BlockSpec(shape, lambda i: (0,) * len(shape)) if grid else vmem()

        if grid:
            specs = [whole_block(a.shape) if s is None else s for s, a in zip(specs, args)]
        else:
            specs = [vmem() if s is None else s for s in specs]
        count = len(args)
        tokens = tuple(after) + (() if self.token is None else (self.token,))
        specs = specs + [pl.BlockSpec(memory_space=pl.ANY)] * len(tokens)
        args = args + tokens
        body = lambda *refs: kernel(*refs[:count], *refs[len(args) :])
        results = pl.pallas_call(
            body,
            grid=(1,) if grid else (),
            in_specs=specs,
            out_specs=[whole_block(shape) for shape in outs],
            out_shape=[jax.ShapeDtypeStruct(shape, F32) for shape in outs],
            scratch_shapes=scratch,
            compiler_params=pltpu.CompilerParams(vmem_limit_bytes=VMEM_LIMIT),
            cost_estimate=pl.CostEstimate(
                flops=int(cost[0]), bytes_accessed=int(cost[1]), transcendentals=0
            ),
        )(*args)
        self.token = results[-1]
        return results


def swap(blocks):
    return [blocks[0]] + [
        lax.ppermute(blocks[d], "mode", [(i, (i + d) % GROUPS) for i in range(GROUPS)])
        for d in range(1, GROUPS)
    ]


def trade(inner, outer):
    pair = [(i, i ^ 1) for i in range(COLUMNS)]
    across = [(i, (i + (1 if i % 2 else -1)) % COLUMNS) for i in range(COLUMNS)]
    return lax.ppermute(inner, "elem", pair), lax.ppermute(outer, "elem", across)


def on_device(velocity, column_width, row_height, disc_mask):
    geometry = (column_width, row_height)
    own = velocity.reshape(3, 2 * NODES, LOCAL)
    table = device_mode_table()
    planes = plane_tables()
    modes = mode_table()
    nodes = node_table()
    gradient = gradient_table()
    run = Program()
    chunks = ((0, 2), (2, 1))

    def block(count):
        return (count * BLOCK, LOCAL)

    def values(count):
        return (count, 2, PAD, HALF) if count > 1 else (2, PAD, HALF)

    def rows_scratch(count):
        return [pltpu.VMEM((count * 4 * PAD, MODES), BF16) for _ in range(2)]

    def modes_scratch(count):
        return [pltpu.VMEM((count * PAD, MODES), F32) for _ in range(2)]

    sent = [
        swap(
            run.call(
                pack_kernel, [component_block(*chunk)], [block(chunk[1])] * GROUPS, [], (1e3, 1e3),
                own, grid=True,
            )
        )
        for chunk in chunks
    ]
    field01, along01, tend01, press = run.call(
        first_kernel,
        [smem()] * 3 + [None] * 11,
        [values(2)] * 3 + [(8, 128)],
        rows_scratch(2),
        (1e3, 1e3),
        *geometry, disc_mask, *sent[0], *planes, gradient, modes, nodes,
    )
    field2, along2, *back01 = run.call(
        second_kernel,
        [None] * 12,
        [values(1)] * 2 + [block(2)] * GROUPS,
        rows_scratch(1) + modes_scratch(2),
        (1e3, 1e3),
        *sent[1], along01, tend01, press, *planes, modes,
    )
    back01 = swap(back01)
    spectrum, edges = (PAD, MODES), (40, MODES)
    re2, im2, *ends = run.call(
        third_kernel,
        [smem()] * 2 + [None] * 13,
        [spectrum, spectrum, edges, edges],
        [pltpu.VMEM(edges, F32), pltpu.VMEM(edges, F32)],
        (1e3, 1e3),
        *geometry, field01, field2, along2, *sent[1], *planes, gradient, modes,
    )
    back2 = swap(
        run.call(
            fourth_kernel,
            [smem()] + [None] * 4,
            [block(1)] * GROUPS,
            modes_scratch(1),
            (1e3, 1e3),
            column_width, re2, im2, *trade(*ends),
            after=back01[1:2],
        )
    )
    scratch = [pltpu.VMEM((NN, ROWS, LOCAL), F32)]
    part, rights, gaps, sums = {}, {}, {}, {}

    def field(count):
        return (2 * count, NN, ROWS, LOCAL)

    def edge(count):
        return (2 * count, N1 - 1, ROWS, LOCAL)

    def right(i, back, after):
        start, count = chunks[i]
        x, *edges = run.call(
            right_kernel,
            [smem()] * 3 + [component_block(start, count)] + [None] * 5,
            [field(count), edge(count), edge(count)],
            [pltpu.VMEM((count, ROWS * ELEM_ROWS, LOCAL), F32)],
            (1e3, 1e3),
            *geometry, disc_mask, own, *back, table,
            grid=True,
            after=after,
        )
        part[i] = (x, *trade(*edges))

    def right_image(i, back):
        start, count = chunks[i]
        rights[i], x, *edges, sums[i] = run.call(
            right_image_kernel,
            [smem()] * 2 + [component_block(start, count)] + [None] * 5,
            [field(count), field(count), edge(count), edge(count), (2 * count, 2, ROWS, LOCAL)],
            [pltpu.VMEM((count, ROWS * ELEM_ROWS, LOCAL), F32)] + scratch,
            (1e3, 1e3),
            *geometry, own, *back, table,
            grid=True,
        )
        part[i] = (x, *trade(*edges))

    def image(i):
        count = chunks[i][1]
        rights[i], x, *edges, sums[i] = run.call(
            image_kernel,
            [smem()] * 2 + [None] * 4,
            [field(count), field(count), edge(count), edge(count), (2 * count, 2, ROWS, LOCAL)],
            scratch,
            (1e3, 1e3),
            *geometry, *part[i], table,
        )
        part[i] = (x, *trade(*edges))

    def product(i, *before):
        start, count = chunks[i]
        gaps[i], total = run.call(
            functools.partial(products_kernel, 2 * start, len(before) > 0),
            [smem()] * 2 + [None] * (6 + len(before)),
            [field(count), (40, LOCAL)],
            scratch,
            (1e3, 1e3),
            *geometry, *part[i], rights[i], sums[i], table, *before,
        )
        return total

    right(0, back01, ())
    image(0)
    right_image(1, back2)
    total = product(0)
    total = product(1, total)
    other = lax.ppermute(total, "elem", [(i, i ^ 1) for i in range(COLUMNS)])
    (spread,) = run.call(
        merge_kernel, [None] * 2, [(CHIPS, 40, LOCAL)], [], (1e3, 1e3), total, other
    )
    everyone = lax.all_to_all(
        spread, "elem", split_axis=0, concat_axis=0, tiled=True,
        axis_index_groups=[[2 * i + core for i in range(CHIPS)] for core in range(2)],
    )
    (result,) = run.call(
        update_kernel,
        [None] * 6,
        [(3, 2 * NODES, LOCAL)],
        [],
        (1e3, 1e3),
        total, everyone, rights[0], gaps[0], rights[1], gaps[1],
    )
    return result.reshape(3, NODES, 2, LOCAL)


def solution(mesh):
    return jax.shard_map(
        on_device,
        mesh=mesh,
        in_specs=(P(None, "elem", None, "mode"), P("elem"), P(), P("elem")),
        out_specs=P(None, "elem", None, "mode"),
        check_vma=False,
    )
```

```python
import functools
import math

import jax
import jax.numpy as jnp
import ml_dtypes
import numpy as np
from jax import lax
from jax.experimental import pallas as pl
from jax.experimental.pallas import tpu as pltpu
from jax.sharding import PartitionSpec as P

ORDER = 8
N1 = ORDER + 1
NN = N1 * N1

gll_points = [
    -1.0,
    -0.8997579954114602,
    -0.6771862795107377,
    -0.3631174638261782,
    0.0,
    0.3631174638261782,
    0.6771862795107377,
    0.8997579954114602,
    1.0,
]
gll_weights = [
    0.0277777777777778,
    0.1654953615608055,
    0.2745387125001617,
    0.3464285109730463,
    0.3715192743764172,
    0.3464285109730463,
    0.2745387125001617,
    0.1654953615608055,
    0.0277777777777778,
]
viscosity = 0.5
time_step = 0.02
thrust_coef = 4.0 / 3.0

MODES = 512
PLANES = 3 * MODES
HALF = PLANES // 2
GROUPS = 4
DISTANCES = (0, 2, 1, 3)
LOCAL = MODES // GROUPS
ROWS = 8
COLUMNS = 32
CHIPS = COLUMNS // 2
NODES = ROWS * NN
SHARE = NODES // GROUPS
ELEM_ROWS = 2 * NN + 2
BLOCK = 2 * ELEM_ROWS
WIDE = BLOCK // 2
SLOT = NN + 1
PAD = 176
TILE = 256
FORWARD = math.sqrt(MODES) / PLANES
DISC_LO = 3 * PLANES // 8
DISC_HI = 5 * PLANES // 8
VMEM_LIMIT = 24 * 1024 * 1024
F32 = jnp.float32
BF16 = jnp.bfloat16


def derivative_matrix():
    points = np.array(gll_points)
    identity = np.eye(9)
    differences = points[:, None] - points[None, :] + identity
    barycentric = 1.0 / np.prod(differences, axis=1)
    off_diagonal = barycentric[None, :] / barycentric[:, None] / differences * (1.0 - identity)
    return off_diagonal - identity * off_diagonal.sum(axis=1)[:, None]


W1 = np.array(gll_weights)
D1 = derivative_matrix()
K1 = (D1.T @ (W1[:, None] * D1)) / W1[:, None]
MULT = np.ones(9)
MULT[0] = MULT[8] = 0.5


def split_table(table):
    table = np.asarray(table, np.float32)
    high = table.astype(ml_dtypes.bfloat16)
    low = (table - high.astype(np.float32)).astype(ml_dtypes.bfloat16)
    return high, low


def plane_tables():
    k = np.arange(MODES)[:, None]
    j = np.arange(HALF)[None, :]
    angle = 2.0 * np.pi / PLANES * ((k * j) % PLANES)
    return [jnp.asarray(t) for t in split_table(np.cos(angle)) + split_table(np.sin(angle))]


def two_elements(matrix):
    table = np.zeros((PAD, PAD))
    for e in range(2):
        at = slice(e * SLOT, e * SLOT + NN)
        table[at, at] = matrix
    return table


def gradient_table():
    one = np.eye(9)
    table = np.concatenate(
        [-two_elements(np.kron(D1, one)), -two_elements(np.kron(one, D1))], axis=0
    )
    return jnp.asarray(np.concatenate(split_table(table), axis=0))


def mode_table():
    k = np.arange(MODES)
    weight = np.where(k == 0, 1.0, 2.0) / math.sqrt(MODES)
    table = np.zeros((8, MODES), np.float32)
    table[0] = weight
    table[1] = weight * 8.0 * k / MODES
    table[2] = (-1.0) ** k - 1.0
    return jnp.asarray(table)


def node_table():
    table = np.zeros((PAD, 128), np.float32)
    for e in range(2):
        table[e * SLOT : e * SLOT + NN] = np.kron(W1, W1)[:, None]
    return jnp.asarray(table)


def device_mode_table():
    k = np.arange(MODES)
    j = np.arange(DISC_LO, DISC_HI)[:, None]
    angle = 2.0 * np.pi / PLANES * ((k[None, :] * j) % PLANES)
    kz = 8.0 * k / MODES
    rows = np.zeros((8, MODES))
    rows[0] = FORWARD * np.cos(angle).sum(axis=0)
    rows[1] = -FORWARD * np.sin(angle).sum(axis=0)
    rows[2] = 1.0 / time_step + viscosity * kz * kz
    table = rows.reshape(8, GROUPS, LOCAL).transpose(1, 0, 2)
    return jnp.asarray(table.astype(np.float32))


def split(value):
    high = value.astype(BF16)
    return jnp.concatenate([high, (value - high.astype(F32)).astype(BF16)], axis=0)


def dot(left, right, transposed=False):
    dims = (((1,), (1 if transposed else 0,)), ((), ()))
    return lax.dot_general(left, right, dims, preferred_element_type=F32)


def dot3(left, right, transposed=False):
    rows = left.shape[0] // 2
    both = dot(left, right[0], transposed)
    return both[:rows] + (both[rows:] + dot(left[:rows], right[1], transposed))


def block_lanes(distance):
    source = lax.rem(lax.axis_index("mode") + GROUPS - distance, GROUPS)
    return pl.ds(pl.multiple_of(source * LOCAL, LOCAL), LOCAL)


def pack_kernel(v_ref, *out_refs):
    me = lax.axis_index("mode")
    for c in range(v_ref.shape[0]):
        for d in range(GROUPS):
            target = lax.rem(me + d, GROUPS)
            for e in range(2):
                base = c * BLOCK + e * ELEM_ROWS
                out_refs[d][pl.ds(base, 2 * NN), :] = v_ref[
                    c, pl.ds((2 * target + e) * 2 * NN, 2 * NN), :
                ]
                out_refs[d][pl.ds(base + 2 * NN, 2), :] = jnp.zeros((2, LOCAL), F32)


def plane_tile(t):
    columns = pl.ds(pl.multiple_of(t * TILE, TILE), TILE)
    plane = lax.broadcasted_iota(jnp.int32, (1, TILE), 1) + t * TILE
    return columns, plane


def element_values(ref):
    me = lax.axis_index("mode")
    first = lax.broadcasted_iota(jnp.int32, (PAD, 1), 0) < SLOT
    return jnp.where(first, ref[2 * me].astype(F32), ref[2 * me + 1].astype(F32))


def load_modes(v_refs, distances, modes_ref, a_ref, b_ref, components):
    zeros = jnp.zeros((PAD - WIDE, LOCAL), F32)
    extra = jnp.zeros((components * 2 * PAD, LOCAL), F32)
    for i, (d, v_ref) in enumerate(zip(distances, v_refs)):
        lanes = block_lanes(d)
        target = pl.ds(i * LOCAL, LOCAL)
        weight = modes_ref[0:1, lanes]
        wave = modes_ref[1:2, lanes]
        a, b = [], []
        for c in range(components):
            re = v_ref[pl.ds(c * BLOCK, WIDE, stride=2), :]
            im = v_ref[pl.ds(c * BLOCK + 1, WIDE, stride=2), :]
            a += [re * weight, zeros, im * wave, zeros]
            b += [im * weight, zeros, re * wave, zeros]
        a = jnp.concatenate(a, axis=0)
        extra = extra + a * modes_ref[2:3, lanes]
        a_ref[:, target] = split(a)
        b_ref[:, target] = split(jnp.concatenate(b, axis=0))
    return jnp.sum(extra, axis=1, keepdims=True)


def packed_rows(ref, distances, columns):
    return jnp.concatenate([ref[block_lanes(d), columns] for d in distances], axis=0)


def early_kernel(
    components, v0_ref, v1_ref, ch_ref, cl_ref, sh_ref, sl_ref, modes_ref,
    even_ref, odd_ref, extra_ref, a_ref, b_ref,
):
    near = DISTANCES[:2]
    extra = load_modes((v0_ref, v1_ref), near, modes_ref, a_ref, b_ref, components)
    extra_ref[...] = jnp.broadcast_to(extra, extra_ref.shape)
    for t in range(HALF // TILE):
        columns, _ = plane_tile(t)
        cos = tuple(packed_rows(ref, near, columns) for ref in (ch_ref, cl_ref))
        sin = tuple(packed_rows(ref, near, columns) for ref in (sh_ref, sl_ref))
        even_ref[:, columns] = dot3(a_ref[...], cos)
        odd_ref[:, columns] = dot3(b_ref[...], sin)


def plane_values(t, even, odd, extra):
    _, plane = plane_tile(t)
    result = []
    for c in range(extra.shape[0] // (2 * PAD)):
        u = slice(2 * c * PAD, (2 * c + 1) * PAD)
        z = slice((2 * c + 1) * PAD, (2 * c + 2) * PAD)
        field = [even[u] - odd[u], even[u] + odd[u]]
        along = [even[z] + odd[z], even[z] - odd[z]]
        if t == 0:
            start = (plane == 0).astype(F32)
            field[1] = field[1] + extra[u] * start
            along[1] = along[1] + extra[z] * start
        result.append((field, along))
    return result


def slope_terms(gradient_ref, field, push_x, push_y):
    high = field.astype(BF16)
    slopes = dot3(gradient_ref[...], (high, (field - high.astype(F32)).astype(BF16)))
    return push_x * slopes[:PAD] + push_y * slopes[PAD:]


def slope_scales(width_ref, height_ref):
    return 2.0 / jnp.full((PAD, 1), width_ref[0]), 2.0 / element_values(height_ref)


def add_modes(t, tends, cos, sin, modes_ref, re_ref, im_ref):
    gather = lambda values: split(jnp.concatenate(values, axis=0))
    re = dot3(gather([low + high for low, high in tends]), cos, True)
    im = dot3(gather([low - high for low, high in tends]), sin, True)
    if t == 0:
        last = jnp.concatenate([high[:, 0:1] for _, high in tends], axis=0)
        re_ref[...] = re + last * modes_ref[2:3, :]
        im_ref[...] = im
    else:
        re_ref[...] += re
        im_ref[...] += im


def store_modes(re_ref, im_ref, out_refs):
    for d in range(GROUPS):
        target = lax.rem(lax.axis_index("mode") + d, GROUPS)
        lanes = pl.ds(pl.multiple_of(target * LOCAL, LOCAL), LOCAL)
        for c in range(re_ref.shape[0] // PAD):
            rows = pl.ds(c * PAD, WIDE)
            out_refs[d][pl.ds(c * BLOCK, WIDE, stride=2), :] = FORWARD * re_ref[rows, lanes]
            out_refs[d][pl.ds(c * BLOCK + 1, WIDE, stride=2), :] = -FORWARD * im_ref[rows, lanes]


def first_kernel(
    width_ref, height_ref, disc_ref, v2_ref, v3_ref, even_ref, odd_ref, extra_ref,
    ch_ref, cl_ref, sh_ref, sl_ref, gradient_ref, modes_ref, nodes_ref,
    field_ref, along_ref, tend_ref, press_ref, a_ref, b_ref,
):
    far = DISTANCES[2:]
    extra = load_modes((v2_ref, v3_ref), far, modes_ref, a_ref, b_ref, 2)
    extra = extra + extra_ref[:, 0:1]
    scale_x, scale_y = slope_scales(width_ref, height_ref)
    heights = element_values(height_ref)
    weight = element_values(disc_ref) * (width_ref[0] * heights / 4.0) * nodes_ref[:, 0:1]
    press_ref[...] = jnp.zeros_like(press_ref)
    for t in range(HALF // TILE):
        columns, plane = plane_tile(t)
        cos = tuple(packed_rows(ref, far, columns) for ref in (ch_ref, cl_ref))
        sin = tuple(packed_rows(ref, far, columns) for ref in (sh_ref, sl_ref))
        even = even_ref[:, columns] + dot3(a_ref[...], cos)
        odd = odd_ref[:, columns] + dot3(b_ref[...], sin)
        values = plane_values(t, even, odd, extra)
        for side in range(2):
            push_x = values[0][0][side] * scale_x
            push_y = values[1][0][side] * scale_y
            for c, (field, along) in enumerate(values):
                field_ref[c, side, :, columns] = field[side]
                along_ref[c, side, :, columns] = along[side]
                tend_ref[c, side, :, columns] = slope_terms(
                    gradient_ref, field[side], push_x, push_y
                )
        low, high = values[0][0]
        in_low = (plane >= DISC_LO).astype(F32)
        in_high = ((plane > PLANES - DISC_HI) | (plane == 0)).astype(F32)
        share = weight * (low * low * in_low + high * high * in_high)
        share = jnp.sum(share.reshape(PAD // 8, 8, TILE), axis=0)
        press_ref[...] += share[:, :128] + share[:, 128:]


def second_kernel(
    v2_ref, v3_ref, even_ref, odd_ref, extra_ref, along01_ref, tend_ref, press_ref,
    ch_ref, cl_ref, sh_ref, sl_ref, modes_ref,
    field_ref, along_ref, o0_ref, o1_ref, o2_ref, o3_ref, a_ref, b_ref, re_ref, im_ref,
):
    out_refs = (o0_ref, o1_ref, o2_ref, o3_ref)
    far = DISTANCES[2:]
    extra = load_modes((v2_ref, v3_ref), far, modes_ref, a_ref, b_ref, 1)
    extra = extra + extra_ref[:, 0:1]
    for t in range(HALF // TILE):
        columns, _ = plane_tile(t)
        cos = (ch_ref[:, columns], cl_ref[:, columns])
        sin = (sh_ref[:, columns], sl_ref[:, columns])
        far_cos = tuple(packed_rows(ref, far, columns) for ref in (ch_ref, cl_ref))
        far_sin = tuple(packed_rows(ref, far, columns) for ref in (sh_ref, sl_ref))
        even = even_ref[:, columns] + dot3(a_ref[...], far_cos)
        odd = odd_ref[:, columns] + dot3(b_ref[...], far_sin)
        ((field, along),) = plane_values(t, even, odd, extra)
        tends = [[None, None], [None, None]]
        for side in range(2):
            field_ref[side, :, columns] = field[side]
            along_ref[side, :, columns] = along[side]
            for c in range(2):
                tends[c][side] = (
                    tend_ref[c, side, :, columns] + field[side] * along01_ref[c, side, :, columns]
                )
        add_modes(t, tends, cos, sin, modes_ref, re_ref, im_ref)
    store_modes(re_ref, im_ref, out_refs)
    for out_ref in out_refs:
        out_ref[pl.ds(2 * NN, 1), :] = jnp.sum(press_ref[...], axis=0, keepdims=True)


def choose_edges(values, inner_ref, outer_ref, at):
    even = lax.rem(lax.axis_index("elem"), 2) == 0
    first, last = values
    inner_ref[at] = jnp.where(even, last, first)
    outer_ref[at] = jnp.where(even, first, last)


def edge_rows(side, part, element):
    return pl.ds((2 * part + element) * N1, N1), element * SLOT + side * (NN - N1)


def third_kernel(
    width_ref, height_ref, field01_ref, field_ref, along_ref, v0_ref, v1_ref, v2_ref, v3_ref,
    ch_ref, cl_ref, sh_ref, sl_ref, gradient_ref, modes_ref,
    re_ref, im_ref, inner_ref, outer_ref, first_ref, last_ref,
):
    scale_x, scale_y = slope_scales(width_ref, height_ref)
    for t in range(HALF // TILE):
        columns, _ = plane_tile(t)
        cos = (ch_ref[:, columns], cl_ref[:, columns])
        sin = (sh_ref[:, columns], sl_ref[:, columns])
        tends = []
        for side in range(2):
            field = field_ref[side, :, columns]
            push_x = field01_ref[0, side, :, columns] * scale_x
            push_y = field01_ref[1, side, :, columns] * scale_y
            tends.append(
                slope_terms(gradient_ref, field, push_x, push_y)
                + field * along_ref[side, :, columns]
            )
        add_modes(t, [tends], cos, sin, modes_ref, re_ref, im_ref)
    for side, edge_ref in enumerate((first_ref, last_ref)):
        edge_ref[...] = jnp.zeros_like(edge_ref)
        for p in range(2):
            for e in range(2):
                rows, start = edge_rows(side, p, e)
                for d, v_ref in zip(DISTANCES, (v0_ref, v1_ref, v2_ref, v3_ref)):
                    edge_ref[rows, block_lanes(d)] = v_ref[pl.ds(2 * start + p, N1, stride=2), :]
                tend = FORWARD * re_ref[pl.ds(start, N1), :] if p == 0 else (
                    -FORWARD * im_ref[pl.ds(start, N1), :]
                )
                edge_ref[rows, :] = (edge_ref[rows, :] * (1.0 / time_step) + tend) * width_ref[0]
    choose_edges((first_ref[...], last_ref[...]), inner_ref, outer_ref, ...)


def fourth_kernel(
    width_ref, re_ref, im_ref, from_inner_ref, from_outer_ref,
    o0_ref, o1_ref, o2_ref, o3_ref, re_sum_ref, im_sum_ref,
):
    even = lax.rem(lax.axis_index("elem"), 2) == 0
    re_sum_ref[...] = re_ref[...]
    im_sum_ref[...] = im_ref[...]
    scale = 1.0 / (FORWARD * jnp.full((N1, MODES), width_ref[0]))
    for side in range(2):
        for p in range(2):
            for e in range(2):
                rows, start = edge_rows(side, p, e)
                inner, outer = from_inner_ref[rows, :], from_outer_ref[rows, :]
                edge = jnp.where(even, inner, outer) if side else jnp.where(even, outer, inner)
                if p == 0:
                    re_sum_ref[pl.ds(start, N1), :] += edge * scale
                else:
                    im_sum_ref[pl.ds(start, N1), :] -= edge * scale
    store_modes(re_sum_ref, im_sum_ref, (o0_ref, o1_ref, o2_ref, o3_ref))


def row_values(height_ref):
    row = lax.broadcasted_iota(jnp.int32, (ROWS, 128), 0)
    value = jnp.zeros((ROWS, 128), F32)
    for r in range(ROWS):
        value = jnp.where(row == r, height_ref[r].astype(F32), value)
    return value


def next_row(value):
    return jnp.roll(value, -1, axis=0)


def right_side(thrusted, width_ref, height_ref, disc_ref, v_ref, blocks, table_ref, b_ref, t_ref):
    me = lax.axis_index("mode")
    heights = row_values(height_ref)
    width = jnp.full((ROWS, 128), width_ref[0])
    if thrusted:
        disc = row_values(disc_ref)
        total = sum(ref[2 * NN : 2 * NN + 1, :] for ref in blocks)
        total = jnp.sum(total, axis=1, keepdims=True)
        area = (DISC_HI - DISC_LO) * width * jnp.sum(disc * heights, axis=0, keepdims=True)
        thrust = -(0.5 * thrust_coef * ORDER) * (total / area) / width * disc
    jacobian = width * heights / 4.0
    for c in range(v_ref.shape[0]):
        for d, block_ref in zip(DISTANCES, blocks):
            source = lax.rem(me + GROUPS - d, GROUPS)
            rows = pl.ds(pl.multiple_of(source * BLOCK, 8), BLOCK)
            t_ref[c, rows, :] = block_ref[pl.ds(c * BLOCK, BLOCK), :]
    for c in range(v_ref.shape[0]):
        for p in range(2):
            q = 2 * c + p
            push = thrust * table_ref[me, p : p + 1, :] if thrusted and c == 0 else None

            def value(a, b):
                at = (a * N1 + b) * 2 + p
                node = v_ref[c, pl.ds(at, ROWS, stride=2 * NN), :] * (1.0 / time_step)
                node = node + t_ref[c, pl.ds(at, ROWS, stride=ELEM_ROWS), :]
                if push is not None:
                    node = node + push
                return node * (jacobian * float(W1[a] * W1[b]))

            for a in range(N1):
                upper = value(a, N1 - 1) + next_row(value(a, 0))
                lower = jnp.roll(upper, 1, axis=0)
                for b in range(N1):
                    node = lower if b == 0 else upper if b == N1 - 1 else value(a, b)
                    b_ref[q, a * N1 + b] = node


def choose_all_edges(x_ref, inner_ref, outer_ref, q):
    for b in range(N1 - 1):
        ends = x_ref[q, b], x_ref[q, (N1 - 1) * N1 + b]
        choose_edges(ends, inner_ref, outer_ref, (q, b))


def right_kernel(
    width_ref, height_ref, disc_ref, v_ref, t0_ref, t1_ref, t2_ref, t3_ref, table_ref,
    b_ref, inner_ref, outer_ref, t_ref,
):
    blocks = (t0_ref, t1_ref, t2_ref, t3_ref)
    right_side(True, width_ref, height_ref, disc_ref, v_ref, blocks, table_ref, b_ref, t_ref)
    for q in range(b_ref.shape[0]):
        choose_all_edges(b_ref, inner_ref, outer_ref, q)


def add_edges(x_ref, inner_ref, outer_ref, q, store_ref):
    even = lax.rem(lax.axis_index("elem"), 2) == 0
    for a in range(1, N1 - 1):
        for b in range(N1):
            store_ref[q, a * N1 + b] = x_ref[q, a * N1 + b]
    for b in range(N1 - 1):
        inner, outer = inner_ref[q, b], outer_ref[q, b]
        for a, edge in ((0, jnp.where(even, outer, inner)), (N1 - 1, jnp.where(even, inner, outer))):
            store_ref[q, a * N1 + b] = x_ref[q, a * N1 + b] + edge
            if b == 0:
                n = a * N1 + N1 - 1
                store_ref[q, n] = x_ref[q, n] + next_row(edge)


def stiff_line(values):
    half = N1 // 2
    even = [values[i] + values[N1 - 1 - i] for i in range(half)] + [values[half]]
    odd = [values[i] - values[N1 - 1 - i] for i in range(half)]
    result = [None] * N1
    for i in range(half + 1):
        total = even[half] * float(K1[i, half])
        for j in range(half):
            total = total + even[j] * float(0.5 * (K1[i, j] + K1[i, N1 - 1 - j]))
        if i == half:
            result[i] = total
        else:
            rest = odd[0] * float(0.5 * (K1[i, 0] - K1[i, N1 - 1]))
            for j in range(1, half):
                rest = rest + odd[j] * float(0.5 * (K1[i, j] - K1[i, N1 - 1 - j]))
            result[i] = total + rest
            result[N1 - 1 - i] = total - rest
    return result


def operator_scales(width_ref, height_ref, table_ref):
    me = lax.axis_index("mode")
    heights = row_values(height_ref)
    width = jnp.full((ROWS, 128), width_ref[0])
    mass = width * heights / 4.0 * table_ref[me, 2:3, :]
    return mass, viscosity * heights / width, viscosity * width / heights


def local_operator(x_ref, q, scratch_ref, scales, emit):
    mass, ratio_x, ratio_y = scales
    for b in range(N1):
        values = [x_ref[q, a * N1 + b] for a in range(N1)]
        for a, stiff in enumerate(stiff_line(values)):
            scratch_ref[a * N1 + b] = mass * values[a] + ratio_x * stiff
    for a in range(N1):
        values = [x_ref[q, a * N1 + b] for b in range(N1)]
        stiff = stiff_line(values)
        emit(
            a,
            values,
            [
                (scratch_ref[a * N1 + b] + ratio_y * stiff[b]) * float(W1[a] * W1[b])
                for b in range(N1)
            ],
        )


def image_side(scales, b_ref, w_ref, inner_ref, outer_ref, sums_ref, scratch_ref, q):
    state = [jnp.zeros((ROWS, 128), F32), jnp.zeros((ROWS, 128), F32)]

    def emit(a, values, image):
        for b in range(N1):
            state[0] = state[0] + values[b] * values[b] * float(MULT[a] * MULT[b])
            state[1] = state[1] + values[b] * image[b]
        upper = image[N1 - 1] + next_row(image[0])
        lower = jnp.roll(upper, 1, axis=0)
        for b in range(N1):
            value = lower if b == 0 else upper if b == N1 - 1 else image[b]
            w_ref[q, a * N1 + b] = value

    local_operator(b_ref, q, scratch_ref, scales, emit)
    choose_all_edges(w_ref, inner_ref, outer_ref, q)
    sums_ref[q, 0] = state[0]
    sums_ref[q, 1] = state[1]


def image_kernel(
    width_ref, height_ref, x_ref, from_inner_ref, from_outer_ref, table_ref,
    b_ref, w_ref, inner_ref, outer_ref, sums_ref, scratch_ref,
):
    scales = operator_scales(width_ref, height_ref, table_ref)

    def part(q, carry):
        add_edges(x_ref, from_inner_ref, from_outer_ref, q, b_ref)
        image_side(scales, b_ref, w_ref, inner_ref, outer_ref, sums_ref, scratch_ref, q)
        return carry

    lax.fori_loop(0, x_ref.shape[0], part, 0)


def right_image_kernel(
    width_ref, height_ref, v_ref, t0_ref, t1_ref, t2_ref, t3_ref, table_ref,
    b_ref, w_ref, inner_ref, outer_ref, sums_ref, t_ref, scratch_ref,
):
    blocks = (t0_ref, t1_ref, t2_ref, t3_ref)
    right_side(False, width_ref, height_ref, None, v_ref, blocks, table_ref, b_ref, t_ref)
    scales = operator_scales(width_ref, height_ref, table_ref)

    def part(q, carry):
        image_side(scales, b_ref, w_ref, inner_ref, outer_ref, sums_ref, scratch_ref, q)
        return carry

    lax.fori_loop(0, b_ref.shape[0], part, 0)


def whole(value):
    return jnp.sum(value, axis=0, keepdims=True)


def products_kernel(
    start, chained, width_ref, height_ref, x_ref, from_inner_ref, from_outer_ref, b_ref, sums_ref, table_ref,
    *rest,
):
    g_ref, out_ref, scratch_ref = rest[-3:]
    scales = operator_scales(width_ref, height_ref, table_ref)
    out_ref[...] = rest[0][...] if chained else jnp.zeros_like(out_ref)

    def part(q, carry):
        add_edges(x_ref, from_inner_ref, from_outer_ref, q, g_ref)
        cross = jnp.zeros((ROWS, 128), F32)
        for n in range(NN):
            cross = cross + b_ref[q, n] * g_ref[q, n] * float(MULT[n // N1] * MULT[n % N1])
        norm = whole(sums_ref[q, 0])
        shift = jnp.where(norm > 0, whole(cross) / norm, 0.0)
        for n in range(NN):
            g_ref[q, n] = g_ref[q, n] - shift * b_ref[q, n]
        state = [jnp.zeros((ROWS, 128), F32) for _ in range(3)]

        def emit(a, values, image):
            for b in range(N1):
                state[0] = state[0] + values[b] * values[b] * float(MULT[a] * MULT[b])
                state[1] = state[1] + values[b] * image[b]
                state[2] = state[2] + b_ref[q, a * N1 + b] * image[b]

        local_operator(g_ref, q, scratch_ref, scales, emit)
        rows = [norm, shift] + [whole(value) for value in state] + [whole(sums_ref[q, 1])]
        for i, row in enumerate(rows):
            out_ref[pl.ds(6 * i + start + q, 1), :] = row
        return carry

    lax.fori_loop(0, x_ref.shape[0], part, 0)


def merged(blocks):
    norm = sum(block[0] for block in blocks)
    shift = sum(block[0] * block[1] for block in blocks) / norm
    shift = jnp.where(norm > 0, shift, 0.0)
    rest, bend, mixed = 0.0, 0.0, 0.0
    for block in blocks:
        gap = block[1] - shift
        rest = rest + (block[2] + gap * gap * block[0])
        bend = bend + (block[3] + gap * (2.0 * block[4] + gap * block[5]))
        mixed = mixed + (block[4] + gap * block[5])
    return norm, shift, rest, bend, mixed, sum(block[5] for block in blocks)


def six(read):
    return [read(pl.ds(6 * i, 6)) for i in range(6)]


def merge_kernel(own_ref, other_ref, out_ref):
    rows = merged([six(lambda at: ref[at, :]) for ref in (own_ref, other_ref)])
    rows = jnp.concatenate(list(rows) + [jnp.zeros((4, 128), F32)], axis=0)
    for d in range(CHIPS):
        out_ref[d] = rows


def update_kernel(own_ref, all_ref, b01_ref, g01_ref, b2_ref, g2_ref, out_ref):
    norm, sigma, rest, bend, _, _ = merged(
        [six(lambda at: all_ref[d, at, :]) for d in range(CHIPS)]
    )
    step = 1.0 / sigma
    norm_next = step * step * rest
    beta = norm_next / norm
    second = norm_next / (step * step * bend - beta * norm_next / step)
    gap = own_ref[pl.ds(6, 6), :] - sigma
    on_b = step + second * (beta - step * gap)
    on_g = -second * step
    for c in range(3):
        b_ref, g_ref = (b01_ref, g01_ref) if c < 2 else (b2_ref, g2_ref)
        for p in range(2):
            q = 2 * c + p
            r = q if c < 2 else p
            left, right = on_b[q : q + 1], on_g[q : q + 1]
            for n in range(NN):
                out_ref[c, pl.ds(2 * n + p, ROWS, stride=2 * NN), :] = (
                    left * b_ref[r, n] + right * g_ref[r, n]
                )


def vmem():
    return pl.BlockSpec(memory_space=pltpu.VMEM)


def smem():
    return pl.BlockSpec(memory_space=pltpu.SMEM)


def component_block(start, count):
    return pl.BlockSpec((count, 2 * NODES, LOCAL), lambda i: (start // count, 0, 0))


class Program:
    def __init__(self):
        self.token = None

    def call(self, kernel, specs, outs, scratch, cost, *args, grid=False, after=()):
        def whole_block(shape):
            return pl.BlockSpec(shape, lambda i: (0,) * len(shape)) if grid else vmem()

        if grid:
            specs = [whole_block(a.shape) if s is None else s for s, a in zip(specs, args)]
        else:
            specs = [vmem() if s is None else s for s in specs]
        count = len(args)
        tokens = tuple(after) + (() if self.token is None else (self.token,))
        specs = specs + [pl.BlockSpec(memory_space=pl.ANY)] * len(tokens)
        args = args + tokens
        body = lambda *refs: kernel(*refs[:count], *refs[len(args) :])
        results = pl.pallas_call(
            body,
            grid=(1,) if grid else (),
            in_specs=specs,
            out_specs=[whole_block(shape) for shape in outs],
            out_shape=[jax.ShapeDtypeStruct(shape, F32) for shape in outs],
            scratch_shapes=scratch,
            compiler_params=pltpu.CompilerParams(vmem_limit_bytes=VMEM_LIMIT),
            cost_estimate=pl.CostEstimate(
                flops=int(cost[0]), bytes_accessed=int(cost[1]), transcendentals=0
            ),
        )(*args)
        self.token = results[-1]
        return results


def swap(blocks):
    return [
        lax.ppermute(blocks[d], "mode", [(i, (i + d) % GROUPS) for i in range(GROUPS)])
        if d
        else blocks[d]
        for d in DISTANCES
    ]


def trade(inner, outer):
    pair = [(i, i ^ 1) for i in range(COLUMNS)]
    across = [(i, (i + (1 if i % 2 else -1)) % COLUMNS) for i in range(COLUMNS)]
    return lax.ppermute(inner, "elem", pair), lax.ppermute(outer, "elem", across)


def on_device(velocity, column_width, row_height, disc_mask):
    geometry = (column_width, row_height)
    own = velocity.reshape(3, 2 * NODES, LOCAL)
    table = device_mode_table()
    planes = plane_tables()
    modes = mode_table()
    nodes = node_table()
    gradient = gradient_table()
    run = Program()
    chunks = ((0, 2), (2, 1))

    def block(count):
        return (count * BLOCK, LOCAL)

    def values(count):
        return (count, 2, PAD, HALF) if count > 1 else (2, PAD, HALF)

    def modes_scratch(count):
        return [pltpu.VMEM((count * PAD, MODES), F32) for _ in range(2)]

    sent = [
        swap(
            run.call(
                pack_kernel, [component_block(*chunk)], [block(chunk[1])] * GROUPS, [], (1e3, 1e3),
                own, grid=True,
            )
        )
        for chunk in chunks
    ]
    def packed_scratch(count):
        return [pltpu.VMEM((count * 4 * PAD, 2 * LOCAL), BF16) for _ in range(2)]

    def early(i):
        count = chunks[i][1]
        rows = 2 * count * PAD
        return run.call(
            functools.partial(early_kernel, count),
            [None] * 7,
            [(rows, HALF), (rows, HALF), (rows, 128)],
            packed_scratch(count),
            (1e3, 1e3),
            *sent[i][:2], *planes, modes,
        )

    early01 = early(0)
    field01, along01, tend01, press = run.call(
        first_kernel,
        [smem()] * 3 + [None] * 12,
        [values(2)] * 3 + [(8, 128)],
        packed_scratch(2),
        (1e3, 1e3),
        *geometry, disc_mask, *sent[0][2:], *early01, *planes, gradient, modes, nodes,
    )
    early2 = early(1)
    field2, along2, *back01 = run.call(
        second_kernel,
        [None] * 13,
        [values(1)] * 2 + [block(2)] * GROUPS,
        packed_scratch(1) + modes_scratch(2),
        (1e3, 1e3),
        *sent[1][2:], *early2, along01, tend01, press, *planes, modes,
    )
    back01 = swap(back01)
    spectrum, edges = (PAD, MODES), (40, MODES)
    re2, im2, *ends = run.call(
        third_kernel,
        [smem()] * 2 + [None] * 13,
        [spectrum, spectrum, edges, edges],
        [pltpu.VMEM(edges, F32), pltpu.VMEM(edges, F32)],
        (1e3, 1e3),
        *geometry, field01, field2, along2, *sent[1], *planes, gradient, modes,
    )
    back2 = swap(
        run.call(
            fourth_kernel,
            [smem()] + [None] * 4,
            [block(1)] * GROUPS,
            modes_scratch(1),
            (1e3, 1e3),
            column_width, re2, im2, *trade(*ends),
            after=back01[1:2],
        )
    )
    scratch = [pltpu.VMEM((NN, ROWS, LOCAL), F32)]
    part, rights, gaps, sums = {}, {}, {}, {}

    def field(count):
        return (2 * count, NN, ROWS, LOCAL)

    def edge(count):
        return (2 * count, N1 - 1, ROWS, LOCAL)

    def right(i, back, after):
        start, count = chunks[i]
        x, *edges = run.call(
            right_kernel,
            [smem()] * 3 + [component_block(start, count)] + [None] * 5,
            [field(count), edge(count), edge(count)],
            [pltpu.VMEM((count, ROWS * ELEM_ROWS, LOCAL), F32)],
            (1e3, 1e3),
            *geometry, disc_mask, own, *back, table,
            grid=True,
            after=after,
        )
        part[i] = (x, *trade(*edges))

    def right_image(i, back):
        start, count = chunks[i]
        rights[i], x, *edges, sums[i] = run.call(
            right_image_kernel,
            [smem()] * 2 + [component_block(start, count)] + [None] * 5,
            [field(count), field(count), edge(count), edge(count), (2 * count, 2, ROWS, LOCAL)],
            [pltpu.VMEM((count, ROWS * ELEM_ROWS, LOCAL), F32)] + scratch,
            (1e3, 1e3),
            *geometry, own, *back, table,
            grid=True,
        )
        part[i] = (x, *trade(*edges))

    def image(i):
        count = chunks[i][1]
        rights[i], x, *edges, sums[i] = run.call(
            image_kernel,
            [smem()] * 2 + [None] * 4,
            [field(count), field(count), edge(count), edge(count), (2 * count, 2, ROWS, LOCAL)],
            scratch,
            (1e3, 1e3),
            *geometry, *part[i], table,
        )
        part[i] = (x, *trade(*edges))

    def product(i, *before):
        start, count = chunks[i]
        gaps[i], total = run.call(
            functools.partial(products_kernel, 2 * start, len(before) > 0),
            [smem()] * 2 + [None] * (6 + len(before)),
            [field(count), (40, LOCAL)],
            scratch,
            (1e3, 1e3),
            *geometry, *part[i], rights[i], sums[i], table, *before,
        )
        return total

    right(0, back01, ())
    image(0)
    right_image(1, back2)
    total = product(0)
    total = product(1, total)
    other = lax.ppermute(total, "elem", [(i, i ^ 1) for i in range(COLUMNS)])
    (spread,) = run.call(
        merge_kernel, [None] * 2, [(CHIPS, 40, LOCAL)], [], (1e3, 1e3), total, other
    )
    everyone = lax.all_to_all(
        spread, "elem", split_axis=0, concat_axis=0, tiled=True,
        axis_index_groups=[[2 * i + core for i in range(CHIPS)] for core in range(2)],
    )
    (result,) = run.call(
        update_kernel,
        [None] * 6,
        [(3, 2 * NODES, LOCAL)],
        [],
        (1e3, 1e3),
        total, everyone, rights[0], gaps[0], rights[1], gaps[1],
    )
    return result.reshape(3, NODES, 2, LOCAL)


def solution(mesh):
    return jax.shard_map(
        on_device,
        mesh=mesh,
        in_specs=(P(None, "elem", None, "mode"), P("elem"), P(), P("elem")),
        out_specs=P(None, "elem", None, "mode"),
        check_vma=False,
    )
```

```python
import functools
import math

import jax
import jax.numpy as jnp
import ml_dtypes
import numpy as np
from jax import lax
from jax.experimental import pallas as pl
from jax.experimental.pallas import tpu as pltpu
from jax.sharding import PartitionSpec as P

ORDER = 8
N1 = ORDER + 1
NN = N1 * N1

gll_points = [
    -1.0,
    -0.8997579954114602,
    -0.6771862795107377,
    -0.3631174638261782,
    0.0,
    0.3631174638261782,
    0.6771862795107377,
    0.8997579954114602,
    1.0,
]
gll_weights = [
    0.0277777777777778,
    0.1654953615608055,
    0.2745387125001617,
    0.3464285109730463,
    0.3715192743764172,
    0.3464285109730463,
    0.2745387125001617,
    0.1654953615608055,
    0.0277777777777778,
]
viscosity = 0.5
time_step = 0.02
thrust_coef = 4.0 / 3.0

MODES = 512
PLANES = 3 * MODES
HALF = PLANES // 2
GROUPS = 4
DISTANCES = (0, 2, 1, 3)
LOCAL = MODES // GROUPS
ROWS = 8
COLUMNS = 32
CHIPS = COLUMNS // 2
NODES = ROWS * NN
SHARE = NODES // GROUPS
ELEM_ROWS = 2 * NN + 2
BLOCK = 2 * ELEM_ROWS
WIDE = BLOCK // 2
SLOT = NN + 1
PAD = 176
TILE = 256
FORWARD = math.sqrt(MODES) / PLANES
DISC_LO = 3 * PLANES // 8
DISC_HI = 5 * PLANES // 8
VMEM_LIMIT = 24 * 1024 * 1024
F32 = jnp.float32
BF16 = jnp.bfloat16


def derivative_matrix():
    points = np.array(gll_points)
    identity = np.eye(9)
    differences = points[:, None] - points[None, :] + identity
    barycentric = 1.0 / np.prod(differences, axis=1)
    off_diagonal = barycentric[None, :] / barycentric[:, None] / differences * (1.0 - identity)
    return off_diagonal - identity * off_diagonal.sum(axis=1)[:, None]


W1 = np.array(gll_weights)
D1 = derivative_matrix()
K1 = (D1.T @ (W1[:, None] * D1)) / W1[:, None]
MULT = np.ones(9)
MULT[0] = MULT[8] = 0.5


def split_table(table):
    table = np.asarray(table, np.float32)
    high = table.astype(ml_dtypes.bfloat16)
    low = (table - high.astype(np.float32)).astype(ml_dtypes.bfloat16)
    return high, low


def plane_tables():
    k = np.arange(MODES)[:, None]
    j = np.arange(HALF)[None, :]
    angle = 2.0 * np.pi / PLANES * ((k * j) % PLANES)
    return [jnp.asarray(t) for t in split_table(np.cos(angle)) + split_table(np.sin(angle))]


def two_elements(matrix):
    table = np.zeros((PAD, PAD))
    for e in range(2):
        at = slice(e * SLOT, e * SLOT + NN)
        table[at, at] = matrix
    return table


def gradient_table():
    one = np.eye(9)
    table = np.concatenate(
        [-two_elements(np.kron(D1, one)), -two_elements(np.kron(one, D1))], axis=0
    )
    return jnp.asarray(np.concatenate(split_table(table), axis=0))


def mode_table():
    k = np.arange(MODES)
    weight = np.where(k == 0, 1.0, 2.0) / math.sqrt(MODES)
    table = np.zeros((8, MODES), np.float32)
    table[0] = weight
    table[1] = weight * 8.0 * k / MODES
    table[2] = (-1.0) ** k - 1.0
    return jnp.asarray(table)


def node_table():
    table = np.zeros((PAD, 128), np.float32)
    for e in range(2):
        table[e * SLOT : e * SLOT + NN] = np.kron(W1, W1)[:, None]
    return jnp.asarray(table)


def device_mode_table():
    k = np.arange(MODES)
    j = np.arange(DISC_LO, DISC_HI)[:, None]
    angle = 2.0 * np.pi / PLANES * ((k[None, :] * j) % PLANES)
    kz = 8.0 * k / MODES
    rows = np.zeros((8, MODES))
    rows[0] = FORWARD * np.cos(angle).sum(axis=0)
    rows[1] = -FORWARD * np.sin(angle).sum(axis=0)
    rows[2] = 1.0 / time_step + viscosity * kz * kz
    table = rows.reshape(8, GROUPS, LOCAL).transpose(1, 0, 2)
    return jnp.asarray(table.astype(np.float32))


def split(value):
    high = value.astype(BF16)
    return jnp.concatenate([high, (value - high.astype(F32)).astype(BF16)], axis=0)


def dot(left, right, transposed=False):
    dims = (((1,), (1 if transposed else 0,)), ((), ()))
    return lax.dot_general(left, right, dims, preferred_element_type=F32)


def dot3(left, right, transposed=False):
    rows = left.shape[0] // 2
    both = dot(left, right[0], transposed)
    return both[:rows] + (both[rows:] + dot(left[:rows], right[1], transposed))


def block_lanes(distance):
    source = lax.rem(lax.axis_index("mode") + GROUPS - distance, GROUPS)
    return pl.ds(pl.multiple_of(source * LOCAL, LOCAL), LOCAL)


def pack_kernel(v_ref, *out_refs):
    me = lax.axis_index("mode")
    for c in range(v_ref.shape[0]):
        for d in range(GROUPS):
            target = lax.rem(me + d, GROUPS)
            for e in range(2):
                base = c * BLOCK + e * ELEM_ROWS
                start = (2 * target + e) * 2 * NN
                for offset, count in ((0, 160), (2 * NN - 8, 8)):
                    out_refs[d][pl.ds(base + offset, count), :] = v_ref[
                        c, pl.ds(start + offset, count), :
                    ]
                out_refs[d][pl.ds(base + 2 * NN, 2), :] = jnp.zeros((2, LOCAL), F32)


def plane_tile(t):
    columns = pl.ds(pl.multiple_of(t * TILE, TILE), TILE)
    plane = lax.broadcasted_iota(jnp.int32, (1, TILE), 1) + t * TILE
    return columns, plane


def element_values(ref):
    me = lax.axis_index("mode")
    first = lax.broadcasted_iota(jnp.int32, (PAD, 1), 0) < SLOT
    return jnp.where(first, ref[2 * me].astype(F32), ref[2 * me + 1].astype(F32))


def load_modes(v_refs, distances, modes_ref, a_ref, b_ref, components):
    zeros = jnp.zeros((PAD - WIDE, LOCAL), F32)
    extra = jnp.zeros((components * 2 * PAD, LOCAL), F32)
    for i, (d, v_ref) in enumerate(zip(distances, v_refs)):
        lanes = block_lanes(d)
        target = pl.ds(i * LOCAL, LOCAL)
        weight = modes_ref[0:1, lanes]
        wave = modes_ref[1:2, lanes]
        a, b = [], []
        for c in range(components):
            re = v_ref[pl.ds(c * BLOCK, WIDE, stride=2), :]
            im = v_ref[pl.ds(c * BLOCK + 1, WIDE, stride=2), :]
            a += [re * weight, zeros, im * wave, zeros]
            b += [im * weight, zeros, re * wave, zeros]
        a = jnp.concatenate(a, axis=0)
        extra = extra + a * modes_ref[2:3, lanes]
        a_ref[:, target] = split(a)
        b_ref[:, target] = split(jnp.concatenate(b, axis=0))
    return jnp.sum(extra, axis=1, keepdims=True)


def packed_rows(ref, distances, columns):
    return jnp.concatenate([ref[block_lanes(d), columns] for d in distances], axis=0)


def early_kernel(
    components, v0_ref, v1_ref, ch_ref, cl_ref, sh_ref, sl_ref, modes_ref,
    even_ref, odd_ref, extra_ref, a_ref, b_ref,
):
    near = DISTANCES[:2]
    extra = load_modes((v0_ref, v1_ref), near, modes_ref, a_ref, b_ref, components)
    extra_ref[...] = jnp.broadcast_to(extra, extra_ref.shape)
    for t in range(HALF // TILE):
        columns, _ = plane_tile(t)
        cos = tuple(packed_rows(ref, near, columns) for ref in (ch_ref, cl_ref))
        sin = tuple(packed_rows(ref, near, columns) for ref in (sh_ref, sl_ref))
        even_ref[:, columns] = dot3(a_ref[...], cos)
        odd_ref[:, columns] = dot3(b_ref[...], sin)


def plane_values(t, even, odd, extra):
    _, plane = plane_tile(t)
    result = []
    for c in range(extra.shape[0] // (2 * PAD)):
        u = slice(2 * c * PAD, (2 * c + 1) * PAD)
        z = slice((2 * c + 1) * PAD, (2 * c + 2) * PAD)
        field = [even[u] - odd[u], even[u] + odd[u]]
        along = [even[z] + odd[z], even[z] - odd[z]]
        if t == 0:
            start = (plane == 0).astype(F32)
            field[1] = field[1] + extra[u] * start
            along[1] = along[1] + extra[z] * start
        result.append((field, along))
    return result


def slope_terms(gradient_ref, field, push_x, push_y):
    high = field.astype(BF16)
    slopes = dot3(gradient_ref[...], (high, (field - high.astype(F32)).astype(BF16)))
    return push_x * slopes[:PAD] + push_y * slopes[PAD:]


def slope_scales(width_ref, height_ref):
    return 2.0 / jnp.full((PAD, 1), width_ref[0]), 2.0 / element_values(height_ref)


def add_modes(t, tends, cos, sin, modes_ref, re_ref, im_ref):
    gather = lambda values: split(jnp.concatenate(values, axis=0))
    re = dot3(gather([low + high for low, high in tends]), cos, True)
    im = dot3(gather([low - high for low, high in tends]), sin, True)
    if t == 0:
        last = jnp.concatenate([high[:, 0:1] for _, high in tends], axis=0)
        re_ref[...] = re + last * modes_ref[2:3, :]
        im_ref[...] = im
    else:
        re_ref[...] += re
        im_ref[...] += im


def store_modes(re_ref, im_ref, out_refs):
    for d in range(GROUPS):
        target = lax.rem(lax.axis_index("mode") + d, GROUPS)
        lanes = pl.ds(pl.multiple_of(target * LOCAL, LOCAL), LOCAL)
        for c in range(re_ref.shape[0] // PAD):
            rows = pl.ds(c * PAD, WIDE)
            out_refs[d][pl.ds(c * BLOCK, WIDE, stride=2), :] = FORWARD * re_ref[rows, lanes]
            out_refs[d][pl.ds(c * BLOCK + 1, WIDE, stride=2), :] = -FORWARD * im_ref[rows, lanes]


def first_kernel(
    width_ref, height_ref, disc_ref, v2_ref, v3_ref, even_ref, odd_ref, extra_ref,
    ch_ref, cl_ref, sh_ref, sl_ref, gradient_ref, modes_ref, nodes_ref,
    field_ref, along_ref, tend_ref, press_ref, a_ref, b_ref,
):
    far = DISTANCES[2:]
    extra = load_modes((v2_ref, v3_ref), far, modes_ref, a_ref, b_ref, 2)
    extra = extra + extra_ref[:, 0:1]
    scale_x, scale_y = slope_scales(width_ref, height_ref)
    heights = element_values(height_ref)
    weight = element_values(disc_ref) * (width_ref[0] * heights / 4.0) * nodes_ref[:, 0:1]
    press_ref[...] = jnp.zeros_like(press_ref)
    for t in range(HALF // TILE):
        columns, plane = plane_tile(t)
        cos = tuple(packed_rows(ref, far, columns) for ref in (ch_ref, cl_ref))
        sin = tuple(packed_rows(ref, far, columns) for ref in (sh_ref, sl_ref))
        even = even_ref[:, columns] + dot3(a_ref[...], cos)
        odd = odd_ref[:, columns] + dot3(b_ref[...], sin)
        values = plane_values(t, even, odd, extra)
        for side in range(2):
            push_x = values[0][0][side] * scale_x
            push_y = values[1][0][side] * scale_y
            for c, (field, along) in enumerate(values):
                field_ref[c, side, :, columns] = field[side]
                along_ref[c, side, :, columns] = along[side]
                tend_ref[c, side, :, columns] = slope_terms(
                    gradient_ref, field[side], push_x, push_y
                )
        low, high = values[0][0]
        in_low = (plane >= DISC_LO).astype(F32)
        in_high = ((plane > PLANES - DISC_HI) | (plane == 0)).astype(F32)
        share = weight * (low * low * in_low + high * high * in_high)
        share = jnp.sum(share.reshape(PAD // 8, 8, TILE), axis=0)
        press_ref[...] += share[:, :128] + share[:, 128:]


def second_kernel(
    v2_ref, v3_ref, even_ref, odd_ref, extra_ref, along01_ref, tend_ref, press_ref,
    ch_ref, cl_ref, sh_ref, sl_ref, modes_ref,
    field_ref, along_ref, o0_ref, o1_ref, o2_ref, o3_ref, a_ref, b_ref, re_ref, im_ref,
):
    out_refs = (o0_ref, o1_ref, o2_ref, o3_ref)
    far = DISTANCES[2:]
    extra = load_modes((v2_ref, v3_ref), far, modes_ref, a_ref, b_ref, 1)
    extra = extra + extra_ref[:, 0:1]
    for t in range(HALF // TILE):
        columns, _ = plane_tile(t)
        cos = (ch_ref[:, columns], cl_ref[:, columns])
        sin = (sh_ref[:, columns], sl_ref[:, columns])
        far_cos = tuple(packed_rows(ref, far, columns) for ref in (ch_ref, cl_ref))
        far_sin = tuple(packed_rows(ref, far, columns) for ref in (sh_ref, sl_ref))
        even = even_ref[:, columns] + dot3(a_ref[...], far_cos)
        odd = odd_ref[:, columns] + dot3(b_ref[...], far_sin)
        ((field, along),) = plane_values(t, even, odd, extra)
        tends = [[None, None], [None, None]]
        for side in range(2):
            field_ref[side, :, columns] = field[side]
            along_ref[side, :, columns] = along[side]
            for c in range(2):
                tends[c][side] = (
                    tend_ref[c, side, :, columns] + field[side] * along01_ref[c, side, :, columns]
                )
        add_modes(t, tends, cos, sin, modes_ref, re_ref, im_ref)
    store_modes(re_ref, im_ref, out_refs)
    for out_ref in out_refs:
        out_ref[pl.ds(2 * NN, 1), :] = jnp.sum(press_ref[...], axis=0, keepdims=True)


def choose_edges(values, inner_ref, outer_ref, at):
    even = lax.rem(lax.axis_index("elem"), 2) == 0
    first, last = values
    inner_ref[at] = jnp.where(even, last, first)
    outer_ref[at] = jnp.where(even, first, last)


def edge_rows(side, part, element):
    return pl.ds((2 * part + element) * N1, N1), element * SLOT + side * (NN - N1)


def third_kernel(
    width_ref, height_ref, field01_ref, field_ref, along_ref, v0_ref, v1_ref, v2_ref, v3_ref,
    ch_ref, cl_ref, sh_ref, sl_ref, gradient_ref, modes_ref,
    re_ref, im_ref, inner_ref, outer_ref, first_ref, last_ref,
):
    scale_x, scale_y = slope_scales(width_ref, height_ref)
    for t in range(HALF // TILE):
        columns, _ = plane_tile(t)
        cos = (ch_ref[:, columns], cl_ref[:, columns])
        sin = (sh_ref[:, columns], sl_ref[:, columns])
        tends = []
        for side in range(2):
            field = field_ref[side, :, columns]
            push_x = field01_ref[0, side, :, columns] * scale_x
            push_y = field01_ref[1, side, :, columns] * scale_y
            tends.append(
                slope_terms(gradient_ref, field, push_x, push_y)
                + field * along_ref[side, :, columns]
            )
        add_modes(t, [tends], cos, sin, modes_ref, re_ref, im_ref)
    for side, edge_ref in enumerate((first_ref, last_ref)):
        edge_ref[...] = jnp.zeros_like(edge_ref)
        for p in range(2):
            for e in range(2):
                rows, start = edge_rows(side, p, e)
                for d, v_ref in zip(DISTANCES, (v0_ref, v1_ref, v2_ref, v3_ref)):
                    edge_ref[rows, block_lanes(d)] = v_ref[pl.ds(2 * start + p, N1, stride=2), :]
                tend = FORWARD * re_ref[pl.ds(start, N1), :] if p == 0 else (
                    -FORWARD * im_ref[pl.ds(start, N1), :]
                )
                edge_ref[rows, :] = (edge_ref[rows, :] * (1.0 / time_step) + tend) * width_ref[0]
    choose_edges((first_ref[...], last_ref[...]), inner_ref, outer_ref, ...)


def fourth_kernel(
    width_ref, re_ref, im_ref, from_inner_ref, from_outer_ref,
    o0_ref, o1_ref, o2_ref, o3_ref, re_sum_ref, im_sum_ref,
):
    even = lax.rem(lax.axis_index("elem"), 2) == 0
    re_sum_ref[...] = re_ref[...]
    im_sum_ref[...] = im_ref[...]
    scale = 1.0 / (FORWARD * jnp.full((N1, MODES), width_ref[0]))
    for side in range(2):
        for p in range(2):
            for e in range(2):
                rows, start = edge_rows(side, p, e)
                inner, outer = from_inner_ref[rows, :], from_outer_ref[rows, :]
                edge = jnp.where(even, inner, outer) if side else jnp.where(even, outer, inner)
                if p == 0:
                    re_sum_ref[pl.ds(start, N1), :] += edge * scale
                else:
                    im_sum_ref[pl.ds(start, N1), :] -= edge * scale
    store_modes(re_sum_ref, im_sum_ref, (o0_ref, o1_ref, o2_ref, o3_ref))


def row_values(height_ref):
    row = lax.broadcasted_iota(jnp.int32, (ROWS, 128), 0)
    value = jnp.zeros((ROWS, 128), F32)
    for r in range(ROWS):
        value = jnp.where(row == r, height_ref[r].astype(F32), value)
    return value


def next_row(value):
    return jnp.roll(value, -1, axis=0)


def right_side(thrusted, width_ref, height_ref, disc_ref, v_ref, blocks, table_ref, b_ref, t_ref):
    me = lax.axis_index("mode")
    heights = row_values(height_ref)
    width = jnp.full((ROWS, 128), width_ref[0])
    if thrusted:
        disc = row_values(disc_ref)
        total = sum(ref[2 * NN : 2 * NN + 1, :] for ref in blocks)
        total = jnp.sum(total, axis=1, keepdims=True)
        area = (DISC_HI - DISC_LO) * width * jnp.sum(disc * heights, axis=0, keepdims=True)
        thrust = -(0.5 * thrust_coef * ORDER) * (total / area) / width * disc
    jacobian = width * heights / 4.0
    for c in range(v_ref.shape[0]):
        for d, block_ref in zip(DISTANCES, blocks):
            source = lax.rem(me + GROUPS - d, GROUPS)
            rows = pl.ds(pl.multiple_of(source * BLOCK, 8), BLOCK)
            t_ref[c, rows, :] = block_ref[pl.ds(c * BLOCK, BLOCK), :]
    for c in range(v_ref.shape[0]):
        for p in range(2):
            q = 2 * c + p
            push = thrust * table_ref[me, p : p + 1, :] if thrusted and c == 0 else None

            def value(a, b):
                at = (a * N1 + b) * 2 + p
                node = v_ref[c, pl.ds(at, ROWS, stride=2 * NN), :] * (1.0 / time_step)
                node = node + t_ref[c, pl.ds(at, ROWS, stride=ELEM_ROWS), :]
                if push is not None:
                    node = node + push
                return node * (jacobian * float(W1[a] * W1[b]))

            for a in range(N1):
                upper = value(a, N1 - 1) + next_row(value(a, 0))
                lower = jnp.roll(upper, 1, axis=0)
                for b in range(N1):
                    node = lower if b == 0 else upper if b == N1 - 1 else value(a, b)
                    b_ref[q, a * N1 + b] = node


def choose_all_edges(x_ref, inner_ref, outer_ref, q):
    for b in range(N1 - 1):
        ends = x_ref[q, b], x_ref[q, (N1 - 1) * N1 + b]
        choose_edges(ends, inner_ref, outer_ref, (q, b))


def right_kernel(
    width_ref, height_ref, disc_ref, v_ref, t0_ref, t1_ref, t2_ref, t3_ref, table_ref,
    b_ref, inner_ref, outer_ref, t_ref,
):
    blocks = (t0_ref, t1_ref, t2_ref, t3_ref)
    right_side(True, width_ref, height_ref, disc_ref, v_ref, blocks, table_ref, b_ref, t_ref)
    for q in range(b_ref.shape[0]):
        choose_all_edges(b_ref, inner_ref, outer_ref, q)


def add_edges(x_ref, inner_ref, outer_ref, q, store_ref):
    even = lax.rem(lax.axis_index("elem"), 2) == 0
    for a in range(1, N1 - 1):
        for b in range(N1):
            store_ref[q, a * N1 + b] = x_ref[q, a * N1 + b]
    for b in range(N1 - 1):
        inner, outer = inner_ref[q, b], outer_ref[q, b]
        for a, edge in ((0, jnp.where(even, outer, inner)), (N1 - 1, jnp.where(even, inner, outer))):
            store_ref[q, a * N1 + b] = x_ref[q, a * N1 + b] + edge
            if b == 0:
                n = a * N1 + N1 - 1
                store_ref[q, n] = x_ref[q, n] + next_row(edge)


def stiff_line(values):
    half = N1 // 2
    even = [values[i] + values[N1 - 1 - i] for i in range(half)] + [values[half]]
    odd = [values[i] - values[N1 - 1 - i] for i in range(half)]
    result = [None] * N1
    for i in range(half + 1):
        total = even[half] * float(K1[i, half])
        for j in range(half):
            total = total + even[j] * float(0.5 * (K1[i, j] + K1[i, N1 - 1 - j]))
        if i == half:
            result[i] = total
        else:
            rest = odd[0] * float(0.5 * (K1[i, 0] - K1[i, N1 - 1]))
            for j in range(1, half):
                rest = rest + odd[j] * float(0.5 * (K1[i, j] - K1[i, N1 - 1 - j]))
            result[i] = total + rest
            result[N1 - 1 - i] = total - rest
    return result


def operator_scales(width_ref, height_ref, table_ref):
    me = lax.axis_index("mode")
    heights = row_values(height_ref)
    width = jnp.full((ROWS, 128), width_ref[0])
    mass = width * heights / 4.0 * table_ref[me, 2:3, :]
    return mass, viscosity * heights / width, viscosity * width / heights


def local_operator(x_ref, q, scratch_ref, scales, emit):
    mass, ratio_x, ratio_y = scales
    for b in range(N1):
        values = [x_ref[q, a * N1 + b] for a in range(N1)]
        for a, stiff in enumerate(stiff_line(values)):
            scratch_ref[a * N1 + b] = mass * values[a] + ratio_x * stiff
    for a in range(N1):
        values = [x_ref[q, a * N1 + b] for b in range(N1)]
        stiff = stiff_line(values)
        emit(
            a,
            values,
            [
                (scratch_ref[a * N1 + b] + ratio_y * stiff[b]) * float(W1[a] * W1[b])
                for b in range(N1)
            ],
        )


def image_side(scales, b_ref, w_ref, inner_ref, outer_ref, sums_ref, scratch_ref, q):
    state = [jnp.zeros((ROWS, 128), F32), jnp.zeros((ROWS, 128), F32)]

    def emit(a, values, image):
        for b in range(N1):
            state[0] = state[0] + values[b] * values[b] * float(MULT[a] * MULT[b])
            state[1] = state[1] + values[b] * image[b]
        upper = image[N1 - 1] + next_row(image[0])
        lower = jnp.roll(upper, 1, axis=0)
        for b in range(N1):
            value = lower if b == 0 else upper if b == N1 - 1 else image[b]
            w_ref[q, a * N1 + b] = value

    local_operator(b_ref, q, scratch_ref, scales, emit)
    choose_all_edges(w_ref, inner_ref, outer_ref, q)
    sums_ref[q, 0] = state[0]
    sums_ref[q, 1] = state[1]


def image_kernel(
    width_ref, height_ref, x_ref, from_inner_ref, from_outer_ref, table_ref,
    b_ref, w_ref, inner_ref, outer_ref, sums_ref, scratch_ref,
):
    scales = operator_scales(width_ref, height_ref, table_ref)

    def part(q, carry):
        add_edges(x_ref, from_inner_ref, from_outer_ref, q, b_ref)
        image_side(scales, b_ref, w_ref, inner_ref, outer_ref, sums_ref, scratch_ref, q)
        return carry

    lax.fori_loop(0, x_ref.shape[0], part, 0)


def right_image_kernel(
    width_ref, height_ref, v_ref, t0_ref, t1_ref, t2_ref, t3_ref, table_ref,
    b_ref, w_ref, inner_ref, outer_ref, sums_ref, t_ref, scratch_ref,
):
    blocks = (t0_ref, t1_ref, t2_ref, t3_ref)
    right_side(False, width_ref, height_ref, None, v_ref, blocks, table_ref, b_ref, t_ref)
    scales = operator_scales(width_ref, height_ref, table_ref)

    def part(q, carry):
        image_side(scales, b_ref, w_ref, inner_ref, outer_ref, sums_ref, scratch_ref, q)
        return carry

    lax.fori_loop(0, b_ref.shape[0], part, 0)


def whole(value):
    return jnp.sum(value, axis=0, keepdims=True)


def products_kernel(
    start, chained, width_ref, height_ref, x_ref, from_inner_ref, from_outer_ref, b_ref, sums_ref, table_ref,
    *rest,
):
    g_ref, out_ref, scratch_ref = rest[-3:]
    scales = operator_scales(width_ref, height_ref, table_ref)
    out_ref[...] = rest[0][...] if chained else jnp.zeros_like(out_ref)

    def part(q, carry):
        add_edges(x_ref, from_inner_ref, from_outer_ref, q, g_ref)
        cross = jnp.zeros((ROWS, 128), F32)
        for n in range(NN):
            cross = cross + b_ref[q, n] * g_ref[q, n] * float(MULT[n // N1] * MULT[n % N1])
        norm = whole(sums_ref[q, 0])
        shift = jnp.where(norm > 0, whole(cross) / norm, 0.0)
        for n in range(NN):
            g_ref[q, n] = g_ref[q, n] - shift * b_ref[q, n]
        state = [jnp.zeros((ROWS, 128), F32) for _ in range(3)]

        def emit(a, values, image):
            for b in range(N1):
                state[0] = state[0] + values[b] * values[b] * float(MULT[a] * MULT[b])
                state[1] = state[1] + values[b] * image[b]
                state[2] = state[2] + b_ref[q, a * N1 + b] * image[b]

        local_operator(g_ref, q, scratch_ref, scales, emit)
        rows = [norm, shift] + [whole(value) for value in state] + [whole(sums_ref[q, 1])]
        for i, row in enumerate(rows):
            out_ref[pl.ds(6 * i + start + q, 1), :] = row
        return carry

    lax.fori_loop(0, x_ref.shape[0], part, 0)


def merged(blocks):
    norm = sum(block[0] for block in blocks)
    shift = sum(block[0] * block[1] for block in blocks) / norm
    shift = jnp.where(norm > 0, shift, 0.0)
    rest, bend, mixed = 0.0, 0.0, 0.0
    for block in blocks:
        gap = block[1] - shift
        rest = rest + (block[2] + gap * gap * block[0])
        bend = bend + (block[3] + gap * (2.0 * block[4] + gap * block[5]))
        mixed = mixed + (block[4] + gap * block[5])
    return norm, shift, rest, bend, mixed, sum(block[5] for block in blocks)


def six(read):
    return [read(pl.ds(6 * i, 6)) for i in range(6)]


def merge_kernel(own_ref, other_ref, out_ref):
    rows = merged([six(lambda at: ref[at, :]) for ref in (own_ref, other_ref)])
    rows = jnp.concatenate(list(rows) + [jnp.zeros((4, 128), F32)], axis=0)
    for d in range(CHIPS):
        out_ref[d] = rows


def update_kernel(own_ref, all_ref, b01_ref, g01_ref, b2_ref, g2_ref, out_ref):
    norm, sigma, rest, bend, _, _ = merged(
        [six(lambda at: all_ref[d, at, :]) for d in range(CHIPS)]
    )
    step = 1.0 / sigma
    norm_next = step * step * rest
    beta = norm_next / norm
    second = norm_next / (step * step * bend - beta * norm_next / step)
    gap = own_ref[pl.ds(6, 6), :] - sigma
    on_b = step + second * (beta - step * gap)
    on_g = -second * step
    for c in range(3):
        b_ref, g_ref = (b01_ref, g01_ref) if c < 2 else (b2_ref, g2_ref)
        for p in range(2):
            q = 2 * c + p
            r = q if c < 2 else p
            left, right = on_b[q : q + 1], on_g[q : q + 1]
            for n in range(NN):
                out_ref[c, pl.ds(2 * n + p, ROWS, stride=2 * NN), :] = (
                    left * b_ref[r, n] + right * g_ref[r, n]
                )


def vmem():
    return pl.BlockSpec(memory_space=pltpu.VMEM)


def smem():
    return pl.BlockSpec(memory_space=pltpu.SMEM)


def component_block(start, count):
    return pl.BlockSpec((count, 2 * NODES, LOCAL), lambda i: (start // count, 0, 0))


class Program:
    def __init__(self):
        self.token = None

    def call(self, kernel, specs, outs, scratch, cost, *args, grid=False, after=()):
        def whole_block(shape):
            return pl.BlockSpec(shape, lambda i: (0,) * len(shape)) if grid else vmem()

        if grid:
            specs = [whole_block(a.shape) if s is None else s for s, a in zip(specs, args)]
        else:
            specs = [vmem() if s is None else s for s in specs]
        count = len(args)
        tokens = tuple(after) + (() if self.token is None else (self.token,))
        specs = specs + [pl.BlockSpec(memory_space=pl.ANY)] * len(tokens)
        args = args + tokens
        body = lambda *refs: kernel(*refs[:count], *refs[len(args) :])
        results = pl.pallas_call(
            body,
            grid=(1,) if grid else (),
            in_specs=specs,
            out_specs=[whole_block(shape) for shape in outs],
            out_shape=[jax.ShapeDtypeStruct(shape, F32) for shape in outs],
            scratch_shapes=scratch,
            compiler_params=pltpu.CompilerParams(vmem_limit_bytes=VMEM_LIMIT),
            cost_estimate=pl.CostEstimate(
                flops=int(cost[0]), bytes_accessed=int(cost[1]), transcendentals=0
            ),
        )(*args)
        self.token = results[-1]
        return results


def swap(blocks):
    return [
        lax.ppermute(blocks[d], "mode", [(i, (i + d) % GROUPS) for i in range(GROUPS)])
        if d
        else blocks[d]
        for d in DISTANCES
    ]


def trade(inner, outer):
    pair = [(i, i ^ 1) for i in range(COLUMNS)]
    across = [(i, (i + (1 if i % 2 else -1)) % COLUMNS) for i in range(COLUMNS)]
    return lax.ppermute(inner, "elem", pair), lax.ppermute(outer, "elem", across)


def on_device(velocity, column_width, row_height, disc_mask):
    geometry = (column_width, row_height)
    own = velocity.reshape(3, 2 * NODES, LOCAL)
    table = device_mode_table()
    planes = plane_tables()
    modes = mode_table()
    nodes = node_table()
    gradient = gradient_table()
    run = Program()
    chunks = ((0, 2), (2, 1))

    def block(count):
        return (count * BLOCK, LOCAL)

    def values(count):
        return (count, 2, PAD, HALF) if count > 1 else (2, PAD, HALF)

    def modes_scratch(count):
        return [pltpu.VMEM((count * PAD, MODES), F32) for _ in range(2)]

    sent = [
        swap(
            run.call(
                pack_kernel, [component_block(*chunk)], [block(chunk[1])] * GROUPS, [], (1e3, 1e3),
                own, grid=True,
            )
        )
        for chunk in chunks
    ]
    def packed_scratch(count):
        return [pltpu.VMEM((count * 4 * PAD, 2 * LOCAL), BF16) for _ in range(2)]

    def early(i):
        count = chunks[i][1]
        rows = 2 * count * PAD
        return run.call(
            functools.partial(early_kernel, count),
            [None] * 7,
            [(rows, HALF), (rows, HALF), (rows, 128)],
            packed_scratch(count),
            (1e3, 1e3),
            *sent[i][:2], *planes, modes,
        )

    early01 = early(0)
    field01, along01, tend01, press = run.call(
        first_kernel,
        [smem()] * 3 + [None] * 12,
        [values(2)] * 3 + [(8, 128)],
        packed_scratch(2),
        (1e3, 1e3),
        *geometry, disc_mask, *sent[0][2:], *early01, *planes, gradient, modes, nodes,
    )
    early2 = early(1)
    field2, along2, *back01 = run.call(
        second_kernel,
        [None] * 13,
        [values(1)] * 2 + [block(2)] * GROUPS,
        packed_scratch(1) + modes_scratch(2),
        (1e3, 1e3),
        *sent[1][2:], *early2, along01, tend01, press, *planes, modes,
    )
    back01 = swap(back01)
    spectrum, edges = (PAD, MODES), (40, MODES)
    re2, im2, *ends = run.call(
        third_kernel,
        [smem()] * 2 + [None] * 13,
        [spectrum, spectrum, edges, edges],
        [pltpu.VMEM(edges, F32), pltpu.VMEM(edges, F32)],
        (1e3, 1e3),
        *geometry, field01, field2, along2, *sent[1], *planes, gradient, modes,
    )
    back2 = swap(
        run.call(
            fourth_kernel,
            [smem()] + [None] * 4,
            [block(1)] * GROUPS,
            modes_scratch(1),
            (1e3, 1e3),
            column_width, re2, im2, *trade(*ends),
            after=back01[1:2],
        )
    )
    scratch = [pltpu.VMEM((NN, ROWS, LOCAL), F32)]
    part, rights, gaps, sums = {}, {}, {}, {}

    def field(count):
        return (2 * count, NN, ROWS, LOCAL)

    def edge(count):
        return (2 * count, N1 - 1, ROWS, LOCAL)

    def right(i, back, after):
        start, count = chunks[i]
        x, *edges = run.call(
            right_kernel,
            [smem()] * 3 + [component_block(start, count)] + [None] * 5,
            [field(count), edge(count), edge(count)],
            [pltpu.VMEM((count, ROWS * ELEM_ROWS, LOCAL), F32)],
            (1e3, 1e3),
            *geometry, disc_mask, own, *back, table,
            grid=True,
            after=after,
        )
        part[i] = (x, *trade(*edges))

    def right_image(i, back):
        start, count = chunks[i]
        rights[i], x, *edges, sums[i] = run.call(
            right_image_kernel,
            [smem()] * 2 + [component_block(start, count)] + [None] * 5,
            [field(count), field(count), edge(count), edge(count), (2 * count, 2, ROWS, LOCAL)],
            [pltpu.VMEM((count, ROWS * ELEM_ROWS, LOCAL), F32)] + scratch,
            (1e3, 1e3),
            *geometry, own, *back, table,
            grid=True,
        )
        part[i] = (x, *trade(*edges))

    def image(i):
        count = chunks[i][1]
        rights[i], x, *edges, sums[i] = run.call(
            image_kernel,
            [smem()] * 2 + [None] * 4,
            [field(count), field(count), edge(count), edge(count), (2 * count, 2, ROWS, LOCAL)],
            scratch,
            (1e3, 1e3),
            *geometry, *part[i], table,
        )
        part[i] = (x, *trade(*edges))

    def product(i, *before):
        start, count = chunks[i]
        gaps[i], total = run.call(
            functools.partial(products_kernel, 2 * start, len(before) > 0),
            [smem()] * 2 + [None] * (6 + len(before)),
            [field(count), (40, LOCAL)],
            scratch,
            (1e3, 1e3),
            *geometry, *part[i], rights[i], sums[i], table, *before,
        )
        return total

    right(0, back01, ())
    image(0)
    right_image(1, back2)
    total = product(0)
    total = product(1, total)
    other = lax.ppermute(total, "elem", [(i, i ^ 1) for i in range(COLUMNS)])
    (spread,) = run.call(
        merge_kernel, [None] * 2, [(CHIPS, 40, LOCAL)], [], (1e3, 1e3), total, other
    )
    everyone = lax.all_to_all(
        spread, "elem", split_axis=0, concat_axis=0, tiled=True,
        axis_index_groups=[[2 * i + core for i in range(CHIPS)] for core in range(2)],
    )
    (result,) = run.call(
        update_kernel,
        [None] * 6,
        [(3, 2 * NODES, LOCAL)],
        [],
        (1e3, 1e3),
        total, everyone, rights[0], gaps[0], rights[1], gaps[1],
    )
    return result.reshape(3, NODES, 2, LOCAL)


def solution(mesh):
    return jax.shard_map(
        on_device,
        mesh=mesh,
        in_specs=(P(None, "elem", None, "mode"), P("elem"), P(), P("elem")),
        out_specs=P(None, "elem", None, "mode"),
        check_vma=False,
    )
```
